256 devices in a mesh: gx: 16 (over y_hi, z), gy: 4 (over y_lo, core), gz: 4 (over x).
Axes of the slice: x: 4, y: 4 (y_hi: 2, y_lo: 2; y = y_hi * 2 + y_lo), z: 8, core: 2. Of those that a mesh axis runs over, the one named last changes fastest.
Arguments:
- snapshot: bfloat16 [32, 16, 128, 512], P(None, 'gx', 'gy', 'gz'), may hold values from -6 to 6
- snap_index: int32 [1], replicated, may hold values from 0 to 63
- snap_means: float32 [64, 32], replicated, may hold values from -0.5 to 0.5
- snap_scales: float32 [64, 32], replicated, may hold values from 0.5 to 2
- out_bias: float32 [32], replicated, may hold values from -3 to 3
- kernel: bfloat16 [32, 32, 3, 3, 3], replicated, may hold values from -0.21875 to 0.21875
- cotangent: bfloat16 [32, 16, 128, 512], P(None, 'gx', 'gy', 'gz'), may hold values from -6 to 6
Outputs:
- predicted: bfloat16 [32, 16, 128, 512], P(None, 'gx', 'gy', 'gz')
- snapshot_grad: bfloat16 [32, 16, 128, 512], P(None, 'gx', 'gy', 'gz')
- kernel_grad: float32 [32, 32, 3, 3, 3], replicated
- bias_grad: float32 [32], replicated
The draws below stay inside these ranges and needn't reach their ends.
All inputs are finite; a program needn't handle non-finite values.
Results may differ from the reference program's by a relative error of at most 0.0046.
Values may be sent and summed in bfloat16 or wider, within the bound.
A program may use at most 64 MiB of HBM per device.

```python
import math
import jax
import jax.numpy as jnp
from jax import lax

C = 32
SNAPS = 64
NX = 16
NY = 128
NZ = 512


def levels(own_key, shape, cuts, low, top_value):
    factor_of = 1.0
    for position, shards_of in cuts:
        steps = jax.random.uniform(jax.random.fold_in(jax.random.fold_in(own_key, 6), position), (shards_of,), jnp.float32, low / len(cuts), top_value / len(cuts))
        factor_of = factor_of * jnp.repeat(jnp.exp(steps), shape[position] // shards_of).reshape((-1,) + (1,) * (len(shape) - 1 - position))
    return factor_of


def bell_draw(key, dims, width, bound, shards=(), held_as=jnp.bfloat16):
    level = levels(key, dims, shards, -0.22, 0.18) if shards else 1.0
    result = jax.random.normal(key, dims, jnp.float32) * width * level
    return jnp.minimum(jnp.maximum(result, -bound), bound).astype(held_as)


def setup_inputs(seed: int = 0) -> dict:
    arg_keys = jax.random.split(jax.random.key(seed), 8)
    return {
        "snapshot": bell_draw(arg_keys[0], (C, NX, NY, NZ), 1.0, 6.0, ((1, 16), (2, 4), (3, 4))),
        "snap_index": jax.random.randint(arg_keys[1], (1,), 0, SNAPS).astype(jnp.int32),
        "snap_means": jnp.clip(jax.random.uniform(arg_keys[2], (SNAPS, C), jnp.float32, -0.5, 0.5), -0.5, 0.5),
        "snap_scales": jnp.clip(jnp.exp(jax.random.uniform(arg_keys[3], (SNAPS, C), jnp.float32, math.log(0.5), math.log(2.0))), 0.5, 2.0),
        "out_bias": bell_draw(arg_keys[4], (C,), 0.5, 3.0, (), jnp.float32),
        "kernel": bell_draw(arg_keys[5], (C, C, 3, 3, 3), (27 * C) ** -0.5, 0.21875),
        "cotangent": bell_draw(arg_keys[6], (C, NX, NY, NZ), 1.0, 6.0, ((1, 16), (2, 4), (3, 4))),
    }


def select_row(table, snap_index):
    stored = table.shape[0]
    one_hot = (jnp.arange(stored, dtype=jnp.int32)[:, None] == snap_index[0]).astype(table.dtype)
    return lax.optimization_barrier(jnp.sum(one_hot * table, 0))

def convolve(field, filters):
    return lax.conv_general_dilated(field[None], filters, (1, 1, 1), 'VALID', dimension_numbers=('NCDHW', 'OIDHW', 'NCDHW'), precision=lax.Precision.HIGHEST)[0]

def reference(snapshot, snap_index, snap_means, snap_scales, out_bias, kernel, cotangent):
    centre = select_row(snap_means, snap_index)[:, None, None, None]
    spread = (1.0 / select_row(snap_scales, snap_index))[:, None, None, None]
    normed = ((snapshot.astype(jnp.float32) - centre) * spread).astype(jnp.bfloat16)
    values = lax.optimization_barrier(normed).astype(jnp.float32)
    wrapped = jnp.pad(values, ((0, 0), (1, 1), (0, 0), (1, 1)), mode='wrap')
    padded = jnp.pad(wrapped, ((0, 0), (0, 0), (1, 1), (0, 0)))
    weights = kernel.astype(jnp.float32)
    total, pull = jax.vjp(convolve, padded, weights)
    predicted = (total + out_bias[:, None, None, None]).astype(jnp.bfloat16)
    grads = cotangent.astype(jnp.float32)
    pad_grad, kernel_sum = pull(grads)
    cropped = pad_grad[:, :, 1:-1, :]
    inner_x = cropped[:, 1:-1]
    inner_x = inner_x.at[:, -1].add(cropped[:, 0])
    inner_x = inner_x.at[:, 0].add(cropped[:, -1])
    folded = inner_x[..., 1:-1]
    folded = folded.at[..., -1].add(inner_x[..., 0])
    folded = folded.at[..., 0].add(inner_x[..., -1])
    snapshot_grad = (folded * spread).astype(jnp.bfloat16)
    factor = 1.0 / math.sqrt(NX * NY * NZ)
    kernel_grad = kernel_sum * factor
    bias_grad = lax.optimization_barrier(jnp.sum(grads, (1, 2, 3))) * factor
    return (predicted, snapshot_grad, kernel_grad, bias_grad)
```

```python
import functools
import math

import jax
import jax.numpy as jnp
from jax import lax
from jax.experimental import pallas as pl
from jax.experimental.pallas import tpu as pltpu
from jax.sharding import PartitionSpec as P

F32 = jnp.float32
BF16 = jnp.bfloat16
MESH = pl.DeviceIdType.MESH
C = 32
ROWS = 32
LANES = 128
TAPS = 9
PLANES = 16
ZS = 8
GROUP = 32
BLOCKS = 36
HALO = 34
TOP, BOTTOM = 0, 33
LEFT, RIGHT = 0, 64


def block(b):
    return pl.ds(b * LANES, LANES)


def kernel(
    scale,
    snap, cot, idx, means, scales, bias, weights,
    o_pred, o_sg, o_kg, o_bias,
    raw_own, raw_n, raw_c, w_raw, flat, xn, xc, d, wp, ws,
    edge, side, edge_in, side_in, pack, pack_in,
    res, out32, out16, kg_acc, kg_own, rs_in, z_own, z_in, ag,
    s_load, s_bulk, r_bulk, s_halo, r_halo, s_pack, r_pack, s_sum, r_sum, s_out,
):
    gx, gy, gz = lax.axis_index("gx"), lax.axis_index("gy"), lax.axis_index("gz")
    ring, high = lax.rem(gx, ZS), gx // ZS
    me = high * 16 + gy * 4 + gz

    def member(k):
        return {"gx": (k // 16) * ZS + ring, "gy": lax.rem(k // 4, 4), "gz": lax.rem(k, 4)}

    def along(k):
        return {"gx": high * ZS + k}

    loads = [
        pltpu.make_async_copy(snap, raw_own.at[0], s_load.at[0]),
        pltpu.make_async_copy(cot, raw_own.at[1], s_load.at[1]),
        pltpu.make_async_copy(weights, w_raw, s_load.at[2]),
    ]
    for copy in loads:
        copy.start()

    next_x = [lax.rem(gx + 1, PLANES), lax.rem(gx + PLANES - 1, PLANES)]
    barrier = pltpu.get_barrier_semaphore()
    for x in next_x:
        pl.semaphore_signal(barrier, inc=1, device_id={"gx": x}, device_id_type=MESH)
    for k in range(1, ZS):
        pl.semaphore_signal(barrier, inc=1, device_id=along(lax.rem(ring + k, ZS)), device_id_type=MESH)
    for k in range(1, GROUP):
        pl.semaphore_signal(barrier, inc=1, device_id=member(lax.rem(me + k, GROUP)), device_id_type=MESH)
    pl.semaphore_wait(barrier, 2 + ZS - 1 + GROUP - 1)

    def bulk(field, source, landing):
        copies = []
        for way in range(2):
            copies.append(
                pltpu.make_async_remote_copy(
                    source, landing.at[way], s_bulk.at[field, way], r_bulk.at[field, way],
                    device_id={"gx": next_x[way]}, device_id_type=MESH,
                )
            )
        return copies

    bulk_n = bulk(0, snap, raw_n)
    for copy in bulk_n:
        copy.start()

    chosen = lax.broadcasted_iota(jnp.int32, means.shape, 1) == idx[...]
    centre = jnp.sum(jnp.where(chosen, means[...], 0.0), 1, keepdims=True)
    spread = 1.0 / jnp.sum(jnp.where(chosen, scales[...], 0.0), 1, keepdims=True)
    centre_b = jnp.broadcast_to(centre, (C, LANES))
    spread_b = jnp.broadcast_to(spread, (C, LANES))
    lane = lax.broadcasted_iota(jnp.int32, (C, LANES), 1)

    def relayout(raw, into, row0, normalise, edges):
        for c in range(0, C, 8):
            flat[pl.ds(c * ROWS, 8 * ROWS), :] = raw[pl.ds(c, 8)].astype(F32).reshape(8 * ROWS, LANES)

        def step(y, carry):
            v = flat[pl.ds(y, C, stride=ROWS), :]
            if normalise:
                v = (v - centre_b) * spread_b
            into[pl.ds(row0, C), pl.ds(pl.multiple_of((y + 1) * LANES, LANES), LANES)] = v.astype(BF16)
            if edges:
                last, first = carry
                last = jnp.where(lane == LEFT + 1 + y, pltpu.roll(v, lax.rem(y + LEFT + 2, LANES), 1), last)
                first = jnp.where(lane == RIGHT + 1 + y, pltpu.roll(v, y + RIGHT + 1, 1), first)
                carry = (last, first)
            return carry

        zero = jnp.zeros((C, LANES), F32)
        return lax.fori_loop(0, ROWS, step, (zero, zero) if edges else 0, unroll=4)

    fields = (xn, xc)
    for f in range(2):
        loads[f].wait()
        last, first = relayout(raw_own.at[f], fields[f], C, f == 0, True)
        side[0, f] = last.astype(BF16)
        side[1, f] = first.astype(BF16)
        edge[0, f] = fields[f][pl.ds(C, C), block(1)]
        edge[1, f] = fields[f][pl.ds(C, C), block(ROWS)]

    halo = []
    for e in range(2):
        y = lax.rem(gy + (3 if e == 0 else 1), 4)
        for k in range(3):
            z = lax.rem(gz + k + 3, 4)
            halo.append(
                pltpu.make_async_remote_copy(
                    edge.at[e], edge_in.at[e, 2 - k], s_halo.at[e, k], r_halo.at[e, 2 - k],
                    device_id={"gy": y, "gz": z}, device_id_type=MESH,
                )
            )
    for k in range(2):
        z = lax.rem(gz + (1 if k == 0 else 3), 4)
        halo.append(
            pltpu.make_async_remote_copy(
                side.at[k], side_in.at[k], s_halo.at[2, k], r_halo.at[2, k],
                device_id={"gz": z}, device_id_type=MESH,
            )
        )
    for copy in halo:
        copy.start()

    loads[2].wait()
    rows_i = lax.broadcasted_iota(jnp.int32, (C, 3 * C), 0)
    cols_i = lax.broadcasted_iota(jnp.int32, (C, 3 * C), 1)
    places = [(cols_i == rows_i + a * C).astype(BF16) for a in range(3)]
    eye = (lax.broadcasted_iota(jnp.int32, (C, C), 0) == lax.broadcasted_iota(jnp.int32, (C, C), 1)).astype(BF16)
    for be in range(TAPS):
        total = jnp.zeros((C, 3 * C), F32)
        for a in range(3):
            total = total + jnp.dot(w_raw[a * TAPS + be], places[a], preferred_element_type=F32)
        wp[pl.ds(be * C, C), :] = total.astype(BF16)
        stack = jnp.concatenate([w_raw[(2 - a) * TAPS + TAPS - 1 - be] for a in range(3)], 0)
        turned = lax.dot_general(eye, stack, (((1,), (1,)), ((), ())), preferred_element_type=F32)
        ws[pl.ds(be * C, C), :] = turned.astype(BF16)
    xn[pl.ds(3 * C, C), :] = jnp.ones((C, BLOCKS * LANES), BF16)

    for copy in halo:
        copy.wait()
    above = (gy > 0).astype(F32)
    below = (gy < 3).astype(F32)
    halo_c = None
    for f in range(2):
        row_top = edge_in[1, 1, f].astype(F32) * above
        row_bottom = edge_in[0, 1, f].astype(F32) * below
        h = side_in[0, f].astype(F32) + side_in[1, f].astype(F32)
        h = jnp.where(lane == LEFT, pltpu.roll(edge_in[1, 0, f].astype(F32) * above, LEFT + 1, 1), h)
        h = jnp.where(lane == LEFT + 33, pltpu.roll(edge_in[0, 0, f].astype(F32) * below, LEFT + 34, 1), h)
        h = jnp.where(lane == RIGHT, pltpu.roll(edge_in[1, 2, f].astype(F32) * above, RIGHT, 1), h)
        h = jnp.where(lane == RIGHT + 33, pltpu.roll(edge_in[0, 2, f].astype(F32) * below, RIGHT + 33, 1), h)
        for i, (b, v) in enumerate(((TOP, row_top), (BOTTOM, row_bottom), (HALO, h))):
            v16 = v.astype(BF16)
            fields[f][pl.ds(C, C), block(b)] = v16
            pack[f, i] = v16
        if f == 1:
            halo_c = h
    packs = []
    for way in range(2):
        packs.append(
            pltpu.make_async_remote_copy(
                pack, pack_in.at[way], s_pack.at[way], r_pack.at[way],
                device_id={"gx": next_x[way]}, device_id_type=MESH,
            )
        )
    for copy in packs:
        copy.start()

    def shifted(r, carry):
        at = pl.ds(pl.multiple_of(r * LANES, LANES), LANES)
        v16 = xc[pl.ds(C, C), at]
        v = v16.astype(F32)
        up = jnp.where(lane == LANES - 1, pltpu.roll(halo_c, LANES - 1 - RIGHT - r, 1), pltpu.roll(v, LANES - 1, 1))
        down = jnp.where(lane == 0, pltpu.roll(halo_c, lax.rem(LANES - LEFT - r, LANES), 1), pltpu.roll(v, 1, 1))
        d[pl.ds(0, C), at] = up.astype(BF16)
        d[pl.ds(C, C), at] = v16
        d[pl.ds(2 * C, C), at] = down.astype(BF16)
        return carry

    lax.fori_loop(0, 34, shifted, 0, unroll=2)

    for way, copy in enumerate(bulk_n):
        copy.wait()
    bulk_c = bulk(1, cot, raw_c)
    for copy in bulk_c:
        copy.start()
    for way in range(2):
        relayout(raw_n.at[way], xn, way * 2 * C, True, False)

    span = 8 * LANES
    kg_acc[...] = jnp.zeros_like(kg_acc)

    def gather(k, carry):
        start = k * span
        left = jnp.concatenate(
            [d[:, pl.ds(pl.multiple_of(start + (2 - b) * LANES, LANES), span)] for b in range(3)], 0
        )
        right = xn[:, pl.ds(pl.multiple_of(start + LANES, LANES), span)]
        kg_acc[...] += lax.dot_general(left, right, (((1,), (1,)), ((), ())), preferred_element_type=F32)
        return carry

    lax.fori_loop(0, ROWS * LANES // span, gather, 0)
    for be in range(TAPS):
        kg_own[:, be, :] = kg_acc[pl.ds(be * C, C), :]

    def spread_out(source, landing, slot, stage, count, mine, device):
        for k in range(1, count):
            peer = lax.rem(mine + count // 2 + k - 1 + (1 if k > count // 2 else 0), count)
            peer = lax.rem(mine + k, count)
            pltpu.make_async_remote_copy(
                source(peer), landing.at[slot], s_sum.at[stage], r_sum.at[stage],
                device_id=device(peer), device_id_type=MESH,
            ).start()

    def arrived(landing, stage, count):
        all_of = landing.at[pl.ds(0, count - 1)]
        pltpu.make_async_copy(all_of, all_of, r_sum.at[stage]).wait()
        pltpu.make_async_copy(all_of, all_of, s_sum.at[stage]).wait()

    spread_out(lambda p: kg_own.at[p], rs_in, me, 0, GROUP, me, member)
    rs_in[me] = kg_own[me]

    def convolve(x, filters, finish, target, field):
        def chunk(k, carry):
            at = pl.ds(pl.multiple_of(k * 4 * LANES, 4 * LANES), 4 * LANES)
            res[:, at] = jnp.dot(filters[...], x[pl.ds(0, 3 * C), at], preferred_element_type=F32)
            return carry

        lax.fori_loop(0, BLOCKS // 4, chunk, 0)

        def of(b, e):
            return pl.ds((b * 3 + e) * C, C)

        left = res[of(0, 0), block(HALO)]
        right = res[of(0, 2), block(HALO)]
        for b in range(1, 3):
            left = left + pltpu.roll(res[of(b, 0), block(HALO)], LANES - b, 1)
            right = right + pltpu.roll(res[of(b, 2), block(HALO)], LANES - b, 1)

        def row(y, carry):
            s = []
            for e in range(3):
                total = None
                for b in range(3):
                    part = res[of(b, e), pl.ds(pl.multiple_of((y + b) * LANES, LANES), LANES)]
                    total = part if total is None else total + part
                s.append(total)
            from_left = jnp.where(lane == 0, pltpu.roll(left, lax.rem(LANES - y, LANES), 1), pltpu.roll(s[0], 1, 1))
            from_right = jnp.where(
                lane == LANES - 1, pltpu.roll(right, LANES - 1 - RIGHT - y, 1), pltpu.roll(s[2], LANES - 1, 1)
            )
            out32[pl.ds(y, C, stride=ROWS), :] = finish(s[1] + from_left + from_right)
            return carry

        lax.fori_loop(0, ROWS, row, 0, unroll=2)
        for c in range(0, C, 8):
            out16[field, pl.ds(c, 8)] = out32[pl.ds(c * ROWS, 8 * ROWS), :].reshape(8, ROWS, LANES).astype(BF16)
        copy = pltpu.make_async_copy(out16.at[field], target, s_out.at[field])
        copy.start()
        return copy

    for copy in packs:
        copy.wait()
    for way in range(2):
        for f in range(2):
            for i, b in enumerate((TOP, BOTTOM, HALO)):
                fields[f][pl.ds(way * 2 * C, C), block(b)] = pack_in[way, f, i]
    zero16 = jnp.zeros((3 * C, LANES), BF16)
    for x in fields:
        x[pl.ds(0, 3 * C), block(BLOCKS - 1)] = zero16

    eye32 = lax.broadcasted_iota(jnp.int32, (C, C), 0) == lax.broadcasted_iota(jnp.int32, (C, C), 1)
    bias_col = jnp.sum(jnp.where(eye32, jnp.broadcast_to(bias[...], (C, C)), 0.0), 1, keepdims=True)
    bias_b = jnp.broadcast_to(bias_col, (C, LANES))
    written = [convolve(xn, wp, lambda v: v + bias_b, o_pred, 0)]

    arrived(rs_in, 0, GROUP)
    total = rs_in[0]
    for k in range(1, GROUP):
        total = total + rs_in[k]
    z_own[...] = total
    spread_out(lambda p: z_own, z_in, ring, 1, ZS, ring, along)
    z_in[ring] = total

    for copy in bulk_c:
        copy.wait()
    for way in range(2):
        relayout(raw_c.at[way], xc, way * 2 * C, False, False)
    written.append(convolve(xc, ws, lambda v: v * spread_b, o_sg, 1))

    arrived(z_in, 1, ZS)
    total = z_in[0]
    for k in range(1, ZS):
        total = total + z_in[k]
    ag[me] = total * scale
    spread_out(lambda p: ag.at[me], ag, me, 2, GROUP, me, member)
    arrived(ag, 2, GROUP)
    for be in range(TAPS):
        v = ag[:, be, :]
        for a in range(3):
            turned = v if a == 0 else pltpu.roll(v, LANES - a * C, 1)
            o_kg[a * TAPS + be] = turned[:, :C]
        if be == 4:
            column = jnp.broadcast_to(v[:, 3 * C : 3 * C + 1], (C, C))
            o_bias[...] = jnp.sum(jnp.where(eye32, column, 0.0), 0, keepdims=True)
    for copy in written:
        copy.wait()


def body(snapshot, snap_index, snap_means, snap_scales, out_bias, weights, cotangent):
    cells = PLANES * 4 * ROWS * 4 * LANES
    scale = 1.0 / math.sqrt(cells)
    shape = jax.ShapeDtypeStruct
    dma = pltpu.SemaphoreType.DMA
    vmem = pltpu.VMEM
    hbm = pl.BlockSpec(memory_space=pl.ANY)
    local = pl.BlockSpec(memory_space=pltpu.VMEM)
    tile = (C, LANES)
    pred, sg, kg, bias = pl.pallas_call(
        functools.partial(kernel, scale),
        out_shape=(
            shape((C, ROWS, LANES), BF16),
            shape((C, ROWS, LANES), BF16),
            shape((27, C, C), F32),
            shape((1, C), F32),
        ),
        in_specs=[hbm, hbm, local, local, local, local, hbm],
        out_specs=(hbm, hbm, local, local),
        scratch_shapes=[
            vmem((2, C, ROWS, LANES), BF16),
            vmem((2, C, ROWS, LANES), BF16),
            vmem((2, C, ROWS, LANES), BF16),
            vmem((27, C, C), BF16),
            vmem((C * ROWS, LANES), F32),
            vmem((4 * C, BLOCKS * LANES), BF16),
            vmem((3 * C, BLOCKS * LANES), BF16),
            vmem((3 * C, BLOCKS * LANES), BF16),
            vmem((TAPS * C, 3 * C), BF16),
            vmem((TAPS * C, 3 * C), BF16),
            vmem((2, 2) + tile, BF16),
            vmem((2, 2) + tile, BF16),
            vmem((2, 3, 2) + tile, BF16),
            vmem((2, 2) + tile, BF16),
            vmem((2, 3) + tile, BF16),
            vmem((2, 2, 3) + tile, BF16),
            vmem((TAPS * C, BLOCKS * LANES), F32),
            vmem((C * ROWS, LANES), F32),
            vmem((2, C, ROWS, LANES), BF16),
            vmem((TAPS * C, LANES), F32),
            vmem((GROUP, TAPS, LANES), F32),
            vmem((GROUP, TAPS, LANES), F32),
            vmem((TAPS, LANES), F32),
            vmem((ZS, TAPS, LANES), F32),
            vmem((GROUP, TAPS, LANES), F32),
            dma((3,)),
            dma((2, 2)),
            dma((2, 2)),
            dma((3, 3)),
            dma((3, 3)),
            dma((2,)),
            dma((2,)),
            dma((3,)),
            dma((3,)),
            dma((2,)),
        ],
        compiler_params=pltpu.CompilerParams(
            collective_id=0, has_side_effects=True, vmem_limit_bytes=32 * 2**20
        ),
    )(
        snapshot.reshape(C, ROWS, LANES),
        cotangent.reshape(C, ROWS, LANES),
        snap_index.reshape(1, 1),
        snap_means.T,
        snap_scales.T,
        out_bias.reshape(1, C),
        weights.transpose(2, 3, 4, 0, 1).reshape(27, C, C),
    )
    return (
        pred.reshape(C, 1, ROWS, LANES),
        sg.reshape(C, 1, ROWS, LANES),
        kg.reshape(3, 3, 3, C, C).transpose(3, 4, 0, 1, 2),
        bias.reshape(C),
    )


def solution(mesh):
    split = P(None, "gx", "gy", "gz")
    in_specs = (split, P(), P(), P(), P(), P(), split)
    out_specs = (split, split, P(), P())
    return jax.shard_map(body, mesh=mesh, in_specs=in_specs, out_specs=out_specs, check_vma=False)
```

```python
import functools
import math

import jax
import jax.numpy as jnp
from jax import lax
from jax.experimental import pallas as pl
from jax.experimental.pallas import tpu as pltpu
from jax.sharding import PartitionSpec as P

F32 = jnp.float32
BF16 = jnp.bfloat16
MESH = pl.DeviceIdType.MESH
C = 32
ROWS = 32
LANES = 128
TAPS = 9
PLANES = 16
ZS = 8
GROUP = 32
BLOCKS = 35
HALF = ROWS // 2
HALO = 34
TOP, BOTTOM = 0, 33
LEFT, RIGHT = 0, 64


def block(b):
    return pl.ds(b * LANES, LANES)


def kernel(
    scale,
    snap, cot, idx_in, means_in, scales_in, bias_in, weights,
    o_pred, o_sg, o_kg, o_bias,
    raw_own, raw_n, raw_c, w_raw, idx, means, scales, bias, flat, xn, xc, d, wp, ws,
    edge, side, edge_in, side_in, pack, pack_in,
    res, out32, out16, kg_acc, kg_own, rs_in, z_own, z_in, ag,
    s_load, s_bulk, r_bulk, s_halo, r_halo, s_pack, r_pack, s_sum, r_sum, s_out,
):
    gx, gy, gz = lax.axis_index("gx"), lax.axis_index("gy"), lax.axis_index("gz")
    ring, high = lax.rem(gx, ZS), gx // ZS
    me = high * 16 + gy * 4 + gz

    def member(k):
        return {"gx": (k // 16) * ZS + ring, "gy": lax.rem(k // 4, 4), "gz": lax.rem(k, 4)}

    def along(k):
        return {"gx": high * ZS + k}

    loads = [
        pltpu.make_async_copy(snap, raw_own.at[0], s_load.at[0]),
        pltpu.make_async_copy(cot, raw_own.at[1], s_load.at[1]),
        pltpu.make_async_copy(weights, w_raw, s_load.at[2]),
        pltpu.make_async_copy(idx_in, idx, s_load.at[3]),
        pltpu.make_async_copy(means_in, means, s_load.at[4]),
        pltpu.make_async_copy(scales_in, scales, s_load.at[5]),
        pltpu.make_async_copy(bias_in, bias, s_load.at[6]),
    ]
    for copy in loads:
        copy.start()

    next_x = [lax.rem(gx + 1, PLANES), lax.rem(gx + PLANES - 1, PLANES)]
    barrier = pltpu.get_barrier_semaphore()
    for x in next_x:
        pl.semaphore_signal(barrier, inc=1, device_id={"gx": x}, device_id_type=MESH)
    for k in range(1, ZS):
        pl.semaphore_signal(barrier, inc=1, device_id=along(lax.rem(ring + k, ZS)), device_id_type=MESH)
    for k in range(1, GROUP):
        pl.semaphore_signal(barrier, inc=1, device_id=member(lax.rem(me + k, GROUP)), device_id_type=MESH)
    pl.semaphore_wait(barrier, 2 + ZS - 1 + GROUP - 1)

    def bulk(field, source, landing):
        copies = []
        for half in range(2):
            for way in range(2):
                copies.append(
                    pltpu.make_async_remote_copy(
                        source.at[:, pl.ds(half * HALF, HALF)], landing.at[way, half],
                        s_bulk.at[field, way, half], r_bulk.at[field, way, half],
                        device_id={"gx": next_x[way]}, device_id_type=MESH,
                    )
                )
        return copies

    bulk_n = bulk(0, snap, raw_n)
    bulk_c = bulk(1, cot, raw_c)
    for copy in bulk_n:
        copy.start()

    for copy in loads[3:]:
        copy.wait()
    chosen = lax.broadcasted_iota(jnp.int32, means.shape, 1) == idx[...]
    centre = jnp.sum(jnp.where(chosen, means[...], 0.0), 1, keepdims=True)
    spread = 1.0 / jnp.sum(jnp.where(chosen, scales[...], 0.0), 1, keepdims=True)
    centre_b = jnp.broadcast_to(centre, (C, LANES))
    spread_b = jnp.broadcast_to(spread, (C, LANES))
    lane = lax.broadcasted_iota(jnp.int32, (C, LANES), 1)

    def relayout(raw, flat, into, row0, start, rows, normalise, edges):
        for c in range(0, C, 8):
            flat[pl.ds(c * rows, 8 * rows), :] = raw[pl.ds(c, 8)].astype(F32).reshape(8 * rows, LANES)
        last = first = jnp.zeros((C, LANES), F32)
        for k in range(rows):
            y = start + k
            v = flat[pl.ds(k, C, stride=rows), :]
            if normalise:
                v = (v - centre_b) * spread_b
            into[pl.ds(row0, C), block(y + 1)] = v.astype(BF16)
            if edges:
                last = jnp.where(lane == LEFT + 1 + y, pltpu.roll(v, y + LEFT + 2, 1), last)
                first = jnp.where(lane == RIGHT + 1 + y, pltpu.roll(v, y + RIGHT + 1, 1), first)
        return last, first

    fields = (xn, xc)
    for f in range(2):
        loads[f].wait()
        last, first = relayout(raw_own.at[f], flat.at[f], fields[f], C, 0, ROWS, f == 0, True)
        side[0, f] = last.astype(BF16)
        side[1, f] = first.astype(BF16)
        edge[0, f] = fields[f][pl.ds(C, C), block(1)]
        edge[1, f] = fields[f][pl.ds(C, C), block(ROWS)]

    halo = []
    for e in range(2):
        y = lax.rem(gy + (3 if e == 0 else 1), 4)
        for k in range(3):
            z = lax.rem(gz + k + 3, 4)
            halo.append(
                pltpu.make_async_remote_copy(
                    edge.at[e], edge_in.at[e, 2 - k], s_halo.at[e, k], r_halo.at[e, 2 - k],
                    device_id={"gy": y, "gz": z}, device_id_type=MESH,
                )
            )
    for k in range(2):
        z = lax.rem(gz + (1 if k == 0 else 3), 4)
        halo.append(
            pltpu.make_async_remote_copy(
                side.at[k], side_in.at[k], s_halo.at[2, k], r_halo.at[2, k],
                device_id={"gz": z}, device_id_type=MESH,
            )
        )
    for copy in halo:
        copy.start()

    loads[2].wait()
    rows_i = lax.broadcasted_iota(jnp.int32, (C, 3 * C), 0)
    cols_i = lax.broadcasted_iota(jnp.int32, (C, 3 * C), 1)
    places = [(cols_i == rows_i + a * C).astype(BF16) for a in range(3)]
    eye = (lax.broadcasted_iota(jnp.int32, (C, C), 0) == lax.broadcasted_iota(jnp.int32, (C, C), 1)).astype(BF16)
    for be in range(TAPS):
        total = jnp.zeros((C, 3 * C), F32)
        for a in range(3):
            total = total + jnp.dot(w_raw[a * TAPS + be], places[a], preferred_element_type=F32)
        wp[pl.ds(be * C, C), :] = total.astype(BF16)
        stack = jnp.concatenate([w_raw[(2 - a) * TAPS + TAPS - 1 - be] for a in range(3)], 0)
        turned = lax.dot_general(eye, stack, (((1,), (1,)), ((), ())), preferred_element_type=F32)
        ws[pl.ds(be * C, C), :] = turned.astype(BF16)
    xn[pl.ds(3 * C, C), :] = jnp.ones((C, BLOCKS * LANES), BF16)

    for copy in halo:
        copy.wait()
    above = (gy > 0).astype(F32)
    below = (gy < 3).astype(F32)
    halo_c = None
    for f in range(2):
        row_top = edge_in[1, 1, f].astype(F32) * above
        row_bottom = edge_in[0, 1, f].astype(F32) * below
        h = side_in[0, f].astype(F32) + side_in[1, f].astype(F32)
        h = jnp.where(lane == LEFT, pltpu.roll(edge_in[1, 0, f].astype(F32) * above, LEFT + 1, 1), h)
        h = jnp.where(lane == LEFT + 33, pltpu.roll(edge_in[0, 0, f].astype(F32) * below, LEFT + 34, 1), h)
        h = jnp.where(lane == RIGHT, pltpu.roll(edge_in[1, 2, f].astype(F32) * above, RIGHT, 1), h)
        h = jnp.where(lane == RIGHT + 33, pltpu.roll(edge_in[0, 2, f].astype(F32) * below, RIGHT + 33, 1), h)
        for i, (b, v) in enumerate(((TOP, row_top), (BOTTOM, row_bottom), (HALO, h))):
            v16 = v.astype(BF16)
            fields[f][pl.ds(C, C), block(b)] = v16
            pack[f, i] = v16
        if f == 1:
            halo_c = h
    packs = []
    for way in range(2):
        packs.append(
            pltpu.make_async_remote_copy(
                pack, pack_in.at[way], s_pack.at[way], r_pack.at[way],
                device_id={"gx": next_x[way]}, device_id_type=MESH,
            )
        )
    for copy in packs:
        copy.start()

    for r in range(ROWS + 2):
        v16 = xc[pl.ds(C, C), block(r)]
        v = v16.astype(F32)
        up = jnp.where(lane == LANES - 1, pltpu.roll(halo_c, LANES - 1 - RIGHT - r, 1), pltpu.roll(v, LANES - 1, 1))
        down = jnp.where(lane == 0, pltpu.roll(halo_c, (LANES - LEFT - r) % LANES, 1), pltpu.roll(v, 1, 1))
        d[pl.ds(0, C), block(r)] = up.astype(BF16)
        d[pl.ds(C, C), block(r)] = v16
        d[pl.ds(2 * C, C), block(r)] = down.astype(BF16)

    span = HALF * LANES
    total = None
    for half in range(2):
        for way in range(2):
            bulk_n[2 * half + way].wait()
        for way in range(2):
            relayout(
                raw_n.at[way, half], flat.at[way, pl.ds(half * C * HALF, C * HALF)],
                xn, way * 2 * C, half * HALF, HALF, True, False,
            )
        start = half * span
        left = jnp.concatenate([d[:, pl.ds(start + (2 - b) * LANES, span)] for b in range(3)], 0)
        right = xn[:, pl.ds(start + LANES, span)]
        part = lax.dot_general(left, right, (((1,), (1,)), ((), ())), preferred_element_type=F32)
        if half == 0:
            kg_acc[...] = part
        else:
            kg_acc[...] += part
    for be in range(TAPS):
        kg_own[:, be, :] = kg_acc[pl.ds(be * C, C), :]

    near = {0: 0, 1: 1, 2: 2, 3: 1}
    steps = [(dy, dc, dx) for dy in range(4) for dc in range(2) for dx in range(4)][1:]
    steps.sort(key=lambda t: -(4 * (near[t[0]] + near[t[2]]) + t[1]))
    y, core = high * 2 + gy // 2, lax.rem(gy, 2)
    group_peers = [
        lax.rem(y + dy, 4) * 8 + lax.rem(core + dc, 2) * 4 + lax.rem(gz + dx, 4) for dy, dc, dx in steps
    ]
    ring_peers = [lax.rem(ring + k, ZS) for k in (4, 3, 5, 2, 6, 1, 7)]

    def spread_out(source, landing, slot, stage, peers, device):
        for peer in peers:
            pltpu.make_async_remote_copy(
                source(peer), landing.at[slot], s_sum.at[stage], r_sum.at[stage],
                device_id=device(peer), device_id_type=MESH,
            ).start()

    def arrived(landing, stage, count):
        all_of = landing.at[pl.ds(0, count - 1)]
        pltpu.make_async_copy(all_of, all_of, r_sum.at[stage]).wait()
        pltpu.make_async_copy(all_of, all_of, s_sum.at[stage]).wait()

    spread_out(lambda p: kg_own.at[p], rs_in, me, 0, group_peers, member)
    for copy in bulk_c[:2]:
        copy.start()
    rs_in[me] = kg_own[me]

    def convolve(x, filters, finish, target, field):
        res[...] = jnp.dot(filters[...], x[pl.ds(0, 3 * C), :], preferred_element_type=F32)

        def of(b, e):
            return pl.ds((b * 3 + e) * C, C)

        left = res[of(0, 0), block(HALO)]
        right = res[of(0, 2), block(HALO)]
        for b in range(1, 3):
            left = left + pltpu.roll(res[of(b, 0), block(HALO)], LANES - b, 1)
            right = right + pltpu.roll(res[of(b, 2), block(HALO)], LANES - b, 1)

        for y in range(ROWS):
            s = [sum(res[of(b, e), block(y + b)] for b in range(3)) for e in range(3)]
            from_left = jnp.where(lane == 0, pltpu.roll(left, (LANES - y) % LANES, 1), pltpu.roll(s[0], 1, 1))
            from_right = jnp.where(
                lane == LANES - 1, pltpu.roll(right, LANES - 1 - RIGHT - y, 1), pltpu.roll(s[2], LANES - 1, 1)
            )
            out32[field, pl.ds(y, C, stride=ROWS), :] = finish(s[1] + from_left + from_right)
        for c in range(0, C, 8):
            out16[field, pl.ds(c, 8)] = out32[field, pl.ds(c * ROWS, 8 * ROWS), :].reshape(8, ROWS, LANES).astype(BF16)
        copy = pltpu.make_async_copy(out16.at[field], target, s_out.at[field])
        copy.start()
        return copy

    for copy in packs:
        copy.wait()
    for way in range(2):
        for f in range(2):
            for i, b in enumerate((TOP, BOTTOM, HALO)):
                fields[f][pl.ds(way * 2 * C, C), block(b)] = pack_in[way, f, i]

    eye32 = lax.broadcasted_iota(jnp.int32, (C, C), 0) == lax.broadcasted_iota(jnp.int32, (C, C), 1)
    bias_col = jnp.sum(jnp.where(eye32, jnp.broadcast_to(bias[...], (C, C)), 0.0), 1, keepdims=True)
    bias_b = jnp.broadcast_to(bias_col, (C, LANES))
    written = [convolve(xn, wp, lambda v: v + bias_b, o_pred, 0)]

    arrived(rs_in, 0, GROUP)
    total = rs_in[0]
    for k in range(1, GROUP):
        total = total + rs_in[k]
    z_own[...] = total
    spread_out(lambda p: z_own, z_in, ring, 1, ring_peers, along)
    for copy in bulk_c[2:]:
        copy.start()
    z_in[ring] = total

    arrived(z_in, 1, ZS)
    total = z_in[0]
    for k in range(1, ZS):
        total = total + z_in[k]
    ag[me] = total * scale
    spread_out(lambda p: ag.at[me], ag, me, 2, group_peers, member)
    for copy in bulk_c:
        copy.wait()
    for way in range(2):
        for half in range(2):
            relayout(
                raw_c.at[way, half], flat.at[way, pl.ds(half * C * HALF, C * HALF)],
                xc, way * 2 * C, half * HALF, HALF, False, False,
            )
    written.append(convolve(xc, ws, lambda v: v * spread_b, o_sg, 1))

    arrived(ag, 2, GROUP)
    for be in range(TAPS):
        v = ag[:, be, :]
        for a in range(3):
            turned = v if a == 0 else pltpu.roll(v, LANES - a * C, 1)
            o_kg[a * TAPS + be] = turned[:, :C]
        if be == 4:
            column = jnp.broadcast_to(v[:, 3 * C : 3 * C + 1], (C, C))
            o_bias[...] = jnp.sum(jnp.where(eye32, column, 0.0), 0, keepdims=True)
    for copy in written:
        copy.wait()


def deliver(pred, sg, kg, bias, o_pred, o_sg, o_kg, o_bias, sems):
    copies = [
        pltpu.make_async_copy(source, target, sems.at[i])
        for i, (source, target) in enumerate(((pred, o_pred), (sg, o_sg), (kg, o_kg), (bias, o_bias)))
    ]
    for copy in copies:
        copy.start()
    for copy in copies:
        copy.wait()


def body(snapshot, snap_index, snap_means, snap_scales, out_bias, weights, cotangent):
    cells = PLANES * 4 * ROWS * 4 * LANES
    scale = 1.0 / math.sqrt(cells)
    shape = jax.ShapeDtypeStruct
    dma = pltpu.SemaphoreType.DMA
    vmem = pltpu.VMEM
    hbm = pl.BlockSpec(memory_space=pltpu.HBM)
    anywhere = pl.BlockSpec(memory_space=pl.ANY)
    local = pl.BlockSpec(memory_space=pltpu.VMEM)
    tile = (C, LANES)
    results = (
        shape((C, ROWS, LANES), BF16),
        shape((C, ROWS, LANES), BF16),
        shape((27, C, C), F32),
        shape((1, C), F32),
    )
    computed = pl.pallas_call(
        functools.partial(kernel, scale),
        out_shape=results,
        in_specs=[hbm] * 7,
        out_specs=(anywhere, anywhere, local, local),
        scratch_shapes=[
            vmem((2, C, ROWS, LANES), BF16),
            vmem((2, 2, C, HALF, LANES), BF16),
            vmem((2, 2, C, HALF, LANES), BF16),
            vmem((27, C, C), BF16),
            vmem((1, 1), jnp.int32),
            vmem((C, 64), F32),
            vmem((C, 64), F32),
            vmem((1, C), F32),
            vmem((2, C * ROWS, LANES), F32),
            vmem((4 * C, BLOCKS * LANES), BF16),
            vmem((3 * C, BLOCKS * LANES), BF16),
            vmem((3 * C, BLOCKS * LANES), BF16),
            vmem((TAPS * C, 3 * C), BF16),
            vmem((TAPS * C, 3 * C), BF16),
            vmem((2, 2) + tile, BF16),
            vmem((2, 2) + tile, BF16),
            vmem((2, 3, 2) + tile, BF16),
            vmem((2, 2) + tile, BF16),
            vmem((2, 3) + tile, BF16),
            vmem((2, 2, 3) + tile, BF16),
            vmem((TAPS * C, BLOCKS * LANES), F32),
            vmem((2, C * ROWS, LANES), F32),
            vmem((2, C, ROWS, LANES), BF16),
            vmem((TAPS * C, LANES), F32),
            vmem((GROUP, TAPS, LANES), F32),
            vmem((GROUP, TAPS, LANES), F32),
            vmem((TAPS, LANES), F32),
            vmem((ZS, TAPS, LANES), F32),
            vmem((GROUP, TAPS, LANES), F32),
            dma((7,)),
            dma((2, 2, 2)),
            dma((2, 2, 2)),
            dma((3, 3)),
            dma((3, 3)),
            dma((2,)),
            dma((2,)),
            dma((3,)),
            dma((3,)),
            dma((2,)),
        ],
        compiler_params=pltpu.CompilerParams(
            collective_id=0, has_side_effects=True, vmem_limit_bytes=60 * 2**20
        ),
    )(
        snapshot.reshape(C, ROWS, LANES),
        cotangent.reshape(C, ROWS, LANES),
        snap_index.reshape(1, 1),
        snap_means.T,
        snap_scales.T,
        out_bias.reshape(1, C),
        weights.transpose(2, 3, 4, 0, 1).reshape(27, C, C),
    )
    pred, sg, kg, bias = pl.pallas_call(
        deliver,
        out_shape=results,
        in_specs=[local] * 4,
        out_specs=(hbm,) * 4,
        scratch_shapes=[dma((4,))],
    )(*computed)
    return (
        pred.reshape(C, 1, ROWS, LANES),
        sg.reshape(C, 1, ROWS, LANES),
        kg.reshape(3, 3, 3, C, C).transpose(3, 4, 0, 1, 2),
        bias.reshape(C),
    )


def solution(mesh):
    split = P(None, "gx", "gy", "gz")
    in_specs = (split, P(), P(), P(), P(), P(), split)
    out_specs = (split, split, P(), P())
    return jax.shard_map(body, mesh=mesh, in_specs=in_specs, out_specs=out_specs, check_vma=False)
```

```python
import functools
import math

import jax
import jax.numpy as jnp
from jax import lax
from jax.experimental import pallas as pl
from jax.experimental.pallas import tpu as pltpu
from jax.sharding import PartitionSpec as P

F32 = jnp.float32
BF16 = jnp.bfloat16
MESH = pl.DeviceIdType.MESH
C = 32
ROWS = 32
LANES = 128
TAPS = 9
PLANES = 16
ZS = 8
GROUP = 32
BLOCKS = 35
HALF = ROWS // 2
HALO = 34
TOP, BOTTOM = 0, 33
LEFT, RIGHT = 0, 64


def block(b):
    return pl.ds(b * LANES, LANES)


def kernel(
    scale,
    snap, cot, idx_in, means_in, scales_in, bias_in, weights,
    o_pred, o_sg, o_sum,
    raw_own, raw_n, raw_c, w_raw, idx, means, scales, bias, flat, xn, xc, d, wp, ws,
    edge, side, edge_in, side_in, pack, pack_in,
    res, out32, out16, kg_acc, kg_own, rs_in, z_own, z_in, total_own,
    s_load, s_bulk, r_bulk, s_halo, r_halo, s_pack, r_pack, s_sum, r_sum, s_out,
):
    gx, gy, gz = lax.axis_index("gx"), lax.axis_index("gy"), lax.axis_index("gz")
    ring, high = lax.rem(gx, ZS), gx // ZS
    me = high * 16 + gy * 4 + gz

    def member(k):
        return {"gx": (k // 16) * ZS + ring, "gy": lax.rem(k // 4, 4), "gz": lax.rem(k, 4)}

    def along(k):
        return {"gx": high * ZS + k}

    loads = [
        pltpu.make_async_copy(snap, raw_own.at[0], s_load.at[0]),
        pltpu.make_async_copy(cot, raw_own.at[1], s_load.at[1]),
        pltpu.make_async_copy(weights, w_raw, s_load.at[2]),
        pltpu.make_async_copy(idx_in, idx, s_load.at[3]),
        pltpu.make_async_copy(means_in, means, s_load.at[4]),
        pltpu.make_async_copy(scales_in, scales, s_load.at[5]),
        pltpu.make_async_copy(bias_in, bias, s_load.at[6]),
    ]
    loads[0].start()

    next_x = [lax.rem(gx + 1, PLANES), lax.rem(gx + PLANES - 1, PLANES)]
    barrier = pltpu.get_barrier_semaphore()
    for x in next_x:
        pl.semaphore_signal(barrier, inc=1, device_id={"gx": x}, device_id_type=MESH)
    for k in range(1, ZS):
        pl.semaphore_signal(barrier, inc=1, device_id=along(lax.rem(ring + k, ZS)), device_id_type=MESH)
    for k in range(1, GROUP):
        pl.semaphore_signal(barrier, inc=1, device_id=member(lax.rem(me + k, GROUP)), device_id_type=MESH)
    pl.semaphore_wait(barrier, 2 + ZS - 1 + GROUP - 1)

    def bulk(field, source, landing):
        copies = []
        for half in range(2):
            for way in range(2):
                copies.append(
                    pltpu.make_async_remote_copy(
                        source.at[:, pl.ds(half * HALF, HALF)], landing.at[way, half],
                        s_bulk.at[field, way, half], r_bulk.at[field, way, half],
                        device_id={"gx": next_x[way]}, device_id_type=MESH,
                    )
                )
        return copies

    bulk_n = bulk(0, snap, raw_n)
    bulk_c = bulk(1, cot, raw_c)
    for copy in bulk_n:
        copy.start()
    for i in (4, 5, 3, 1, 2, 6):
        loads[i].start()

    for copy in loads[3:]:
        copy.wait()
    chosen = lax.broadcasted_iota(jnp.int32, means.shape, 1) == idx[...]
    centre = jnp.sum(jnp.where(chosen, means[...], 0.0), 1, keepdims=True)
    spread = 1.0 / jnp.sum(jnp.where(chosen, scales[...], 0.0), 1, keepdims=True)
    centre_b = jnp.broadcast_to(centre, (C, LANES))
    spread_b = jnp.broadcast_to(spread, (C, LANES))
    lane = lax.broadcasted_iota(jnp.int32, (C, LANES), 1)

    def relayout(raw, flat, into, row0, start, rows, normalise, edges):
        for c in range(0, C, 8):
            flat[pl.ds(c * rows, 8 * rows), :] = raw[pl.ds(c, 8)].astype(F32).reshape(8 * rows, LANES)
        last = first = jnp.zeros((C, LANES), F32)
        for k in range(rows):
            y = start + k
            v = flat[pl.ds(k, C, stride=rows), :]
            if normalise:
                v = (v - centre_b) * spread_b
            into[pl.ds(row0, C), block(y + 1)] = v.astype(BF16)
            if edges:
                last = jnp.where(lane == LEFT + 1 + y, pltpu.roll(v, y + LEFT + 2, 1), last)
                first = jnp.where(lane == RIGHT + 1 + y, pltpu.roll(v, y + RIGHT + 1, 1), first)
        return last, first

    fields = (xn, xc)
    for f in range(2):
        loads[f].wait()
        last, first = relayout(raw_own.at[f], flat.at[f], fields[f], C, 0, ROWS, f == 0, True)
        side[0, f] = last.astype(BF16)
        side[1, f] = first.astype(BF16)
        edge[0, f] = fields[f][pl.ds(C, C), block(1)]
        edge[1, f] = fields[f][pl.ds(C, C), block(ROWS)]

    halo = []
    for e in range(2):
        y = lax.rem(gy + (3 if e == 0 else 1), 4)
        for k in range(3):
            z = lax.rem(gz + k + 3, 4)
            halo.append(
                pltpu.make_async_remote_copy(
                    edge.at[e], edge_in.at[e, 2 - k], s_halo.at[e, k], r_halo.at[e, 2 - k],
                    device_id={"gy": y, "gz": z}, device_id_type=MESH,
                )
            )
    for k in range(2):
        z = lax.rem(gz + (1 if k == 0 else 3), 4)
        halo.append(
            pltpu.make_async_remote_copy(
                side.at[k], side_in.at[k], s_halo.at[2, k], r_halo.at[2, k],
                device_id={"gz": z}, device_id_type=MESH,
            )
        )
    for copy in halo:
        copy.start()

    loads[2].wait()
    rows_i = lax.broadcasted_iota(jnp.int32, (C, 3 * C), 0)
    cols_i = lax.broadcasted_iota(jnp.int32, (C, 3 * C), 1)
    places = [(cols_i == rows_i + a * C).astype(BF16) for a in range(3)]
    eye = (lax.broadcasted_iota(jnp.int32, (C, C), 0) == lax.broadcasted_iota(jnp.int32, (C, C), 1)).astype(BF16)
    for be in range(TAPS):
        total = jnp.zeros((C, 3 * C), F32)
        for a in range(3):
            total = total + jnp.dot(w_raw[a * TAPS + be], places[a], preferred_element_type=F32)
        wp[pl.ds(be * C, C), :] = total.astype(BF16)
        stack = jnp.concatenate([w_raw[(2 - a) * TAPS + TAPS - 1 - be] for a in range(3)], 0)
        turned = lax.dot_general(eye, stack, (((1,), (1,)), ((), ())), preferred_element_type=F32)
        ws[pl.ds(be * C, C), :] = turned.astype(BF16)
    xn[pl.ds(3 * C, C), :] = jnp.ones((C, BLOCKS * LANES), BF16)

    for copy in halo:
        copy.wait()
    above = (gy > 0).astype(F32)
    below = (gy < 3).astype(F32)
    halo_c = None
    for f in range(2):
        row_top = edge_in[1, 1, f].astype(F32) * above
        row_bottom = edge_in[0, 1, f].astype(F32) * below
        h = side_in[0, f].astype(F32) + side_in[1, f].astype(F32)
        h = jnp.where(lane == LEFT, pltpu.roll(edge_in[1, 0, f].astype(F32) * above, LEFT + 1, 1), h)
        h = jnp.where(lane == LEFT + 33, pltpu.roll(edge_in[0, 0, f].astype(F32) * below, LEFT + 34, 1), h)
        h = jnp.where(lane == RIGHT, pltpu.roll(edge_in[1, 2, f].astype(F32) * above, RIGHT, 1), h)
        h = jnp.where(lane == RIGHT + 33, pltpu.roll(edge_in[0, 2, f].astype(F32) * below, RIGHT + 33, 1), h)
        for i, (b, v) in enumerate(((TOP, row_top), (BOTTOM, row_bottom), (HALO, h))):
            v16 = v.astype(BF16)
            fields[f][pl.ds(C, C), block(b)] = v16
            pack[f, i] = v16
        if f == 1:
            halo_c = h
    packs = []
    for way in range(2):
        packs.append(
            pltpu.make_async_remote_copy(
                pack, pack_in.at[way], s_pack.at[way], r_pack.at[way],
                device_id={"gx": next_x[way]}, device_id_type=MESH,
            )
        )
    for copy in packs:
        copy.start()

    for r in range(ROWS + 2):
        v16 = xc[pl.ds(C, C), block(r)]
        v = v16.astype(F32)
        up = jnp.where(lane == LANES - 1, pltpu.roll(halo_c, LANES - 1 - RIGHT - r, 1), pltpu.roll(v, LANES - 1, 1))
        down = jnp.where(lane == 0, pltpu.roll(halo_c, (LANES - LEFT - r) % LANES, 1), pltpu.roll(v, 1, 1))
        d[pl.ds(0, C), block(r)] = up.astype(BF16)
        d[pl.ds(C, C), block(r)] = v16
        d[pl.ds(2 * C, C), block(r)] = down.astype(BF16)

    span = HALF * LANES
    total = None
    for half in range(2):
        for way in range(2):
            bulk_n[2 * half + way].wait()
        for way in range(2):
            relayout(
                raw_n.at[way, half], flat.at[way, pl.ds(half * C * HALF, C * HALF)],
                xn, way * 2 * C, half * HALF, HALF, True, False,
            )
        start = half * span
        left = jnp.concatenate([d[:, pl.ds(start + (2 - b) * LANES, span)] for b in range(3)], 0)
        right = xn[:, pl.ds(start + LANES, span)]
        part = lax.dot_general(left, right, (((1,), (1,)), ((), ())), preferred_element_type=F32)
        if half == 0:
            kg_acc[...] = part
        else:
            kg_acc[...] += part
    for be in range(TAPS):
        kg_own[:, be, :] = kg_acc[pl.ds(be * C, C), :]

    near = {0: 0, 1: 1, 2: 2, 3: 1}
    steps = [(dy, dc, dx) for dy in range(4) for dc in range(2) for dx in range(4)][1:]
    steps.sort(key=lambda t: -(4 * (near[t[0]] + near[t[2]]) + t[1]))
    y, core = high * 2 + gy // 2, lax.rem(gy, 2)
    group_peers = [
        lax.rem(y + dy, 4) * 8 + lax.rem(core + dc, 2) * 4 + lax.rem(gz + dx, 4) for dy, dc, dx in steps
    ]
    ring_peers = [lax.rem(ring + k, ZS) for k in (4, 3, 5, 2, 6, 1, 7)]

    def spread_out(source, landing, slot, stage, peers, device):
        for peer in peers:
            pltpu.make_async_remote_copy(
                source(peer), landing.at[slot], s_sum.at[stage], r_sum.at[stage],
                device_id=device(peer), device_id_type=MESH,
            ).start()

    def arrived(landing, stage, count):
        all_of = landing.at[pl.ds(0, count - 1)]
        pltpu.make_async_copy(all_of, all_of, r_sum.at[stage]).wait()
        pltpu.make_async_copy(all_of, all_of, s_sum.at[stage]).wait()

    spread_out(lambda p: kg_own.at[p], rs_in, me, 0, group_peers, member)
    for copy in bulk_c[:2]:
        copy.start()
    rs_in[me] = kg_own[me]

    def convolve(x, filters, finish, target, field):
        res[...] = jnp.dot(filters[...], x[pl.ds(0, 3 * C), :], preferred_element_type=F32)

        def of(b, e):
            return pl.ds((b * 3 + e) * C, C)

        left = res[of(0, 0), block(HALO)]
        right = res[of(0, 2), block(HALO)]
        for b in range(1, 3):
            left = left + pltpu.roll(res[of(b, 0), block(HALO)], LANES - b, 1)
            right = right + pltpu.roll(res[of(b, 2), block(HALO)], LANES - b, 1)

        for y in range(ROWS):
            s = [sum(res[of(b, e), block(y + b)] for b in range(3)) for e in range(3)]
            from_left = jnp.where(lane == 0, pltpu.roll(left, (LANES - y) % LANES, 1), pltpu.roll(s[0], 1, 1))
            from_right = jnp.where(
                lane == LANES - 1, pltpu.roll(right, LANES - 1 - RIGHT - y, 1), pltpu.roll(s[2], LANES - 1, 1)
            )
            out32[field, pl.ds(y, C, stride=ROWS), :] = finish(s[1] + from_left + from_right)
        for c in range(0, C, 8):
            out16[field, pl.ds(c, 8)] = out32[field, pl.ds(c * ROWS, 8 * ROWS), :].reshape(8, ROWS, LANES).astype(BF16)
        copy = pltpu.make_async_copy(out16.at[field], target, s_out.at[field])
        copy.start()
        return copy

    for copy in packs:
        copy.wait()
    for way in range(2):
        for f in range(2):
            for i, b in enumerate((TOP, BOTTOM, HALO)):
                fields[f][pl.ds(way * 2 * C, C), block(b)] = pack_in[way, f, i]

    eye32 = lax.broadcasted_iota(jnp.int32, (C, C), 0) == lax.broadcasted_iota(jnp.int32, (C, C), 1)
    bias_col = jnp.sum(jnp.where(eye32, jnp.broadcast_to(bias[...], (C, C)), 0.0), 1, keepdims=True)
    bias_b = jnp.broadcast_to(bias_col, (C, LANES))
    written = [convolve(xn, wp, lambda v: v + bias_b, o_pred, 0)]

    arrived(rs_in, 0, GROUP)
    total = rs_in[0]
    for k in range(1, GROUP):
        total = total + rs_in[k]
    z_own[...] = total
    spread_out(lambda p: z_own, z_in, ring, 1, ring_peers, along)
    for copy in bulk_c[2:]:
        copy.start()
    z_in[ring] = total

    arrived(z_in, 1, ZS)
    total = z_in[0]
    for k in range(1, ZS):
        total = total + z_in[k]
    total_own[...] = total * scale
    spread_out(lambda p: total_own, o_sum, me, 2, group_peers, member)
    mine = pltpu.make_async_copy(total_own, o_sum.at[me], s_out.at[2])
    mine.start()
    for copy in bulk_c:
        copy.wait()
    for way in range(2):
        for half in range(2):
            relayout(
                raw_c.at[way, half], flat.at[way, pl.ds(half * C * HALF, C * HALF)],
                xc, way * 2 * C, half * HALF, HALF, False, False,
            )
    written.append(convolve(xc, ws, lambda v: v * spread_b, o_sg, 1))

    arrived(o_sum, 2, GROUP)
    mine.wait()
    for copy in written:
        copy.wait()


def deliver(pred, sg, sums, o_pred, o_sg, o_kg, o_bias, pred_v, sg_v, sums_v, kg_v, bias_v, s_in, s_out):
    arrivals = [
        pltpu.make_async_copy(source, target, s_in.at[i])
        for i, (source, target) in enumerate(((sums, sums_v), (pred, pred_v), (sg, sg_v)))
    ]
    for copy in arrivals:
        copy.start()
    departures = [
        pltpu.make_async_copy(source, target, s_out.at[i])
        for i, (source, target) in enumerate(((kg_v, o_kg), (pred_v, o_pred), (sg_v, o_sg), (bias_v, o_bias)))
    ]
    arrivals[0].wait()
    for be in range(TAPS):
        v = sums_v[:, be, :]
        for a in range(3):
            turned = v if a == 0 else pltpu.roll(v, LANES - a * C, 1)
            kg_v[a * TAPS + be] = turned[:, :C]
        if be == 4:
            column = jnp.broadcast_to(v[:, 3 * C : 3 * C + 1], (C, C))
            diagonal = lax.broadcasted_iota(jnp.int32, (C, C), 0) == lax.broadcasted_iota(jnp.int32, (C, C), 1)
            bias_v[...] = jnp.sum(jnp.where(diagonal, column, 0.0), 0, keepdims=True)
    departures[0].start()
    departures[3].start()
    for i in (1, 2):
        arrivals[i].wait()
        departures[i].start()
    for copy in departures:
        copy.wait()


def body(snapshot, snap_index, snap_means, snap_scales, out_bias, weights, cotangent):
    cells = PLANES * 4 * ROWS * 4 * LANES
    scale = 1.0 / math.sqrt(cells)
    shape = jax.ShapeDtypeStruct
    dma = pltpu.SemaphoreType.DMA
    vmem = pltpu.VMEM
    hbm = pl.BlockSpec(memory_space=pltpu.HBM)
    anywhere = pl.BlockSpec(memory_space=pl.ANY)
    tile = (C, LANES)
    results = (
        shape((C, ROWS, LANES), BF16),
        shape((C, ROWS, LANES), BF16),
        shape((27, C, C), F32),
        shape((1, C), F32),
    )
    computed = pl.pallas_call(
        functools.partial(kernel, scale),
        out_shape=results[:2] + (shape((GROUP, TAPS, LANES), F32),),
        in_specs=[hbm] * 7,
        out_specs=(anywhere,) * 3,
        scratch_shapes=[
            vmem((2, C, ROWS, LANES), BF16),
            vmem((2, 2, C, HALF, LANES), BF16),
            vmem((2, 2, C, HALF, LANES), BF16),
            vmem((27, C, C), BF16),
            vmem((1, 1), jnp.int32),
            vmem((C, 64), F32),
            vmem((C, 64), F32),
            vmem((1, C), F32),
            vmem((2, C * ROWS, LANES), F32),
            vmem((4 * C, BLOCKS * LANES), BF16),
            vmem((3 * C, BLOCKS * LANES), BF16),
            vmem((3 * C, BLOCKS * LANES), BF16),
            vmem((TAPS * C, 3 * C), BF16),
            vmem((TAPS * C, 3 * C), BF16),
            vmem((2, 2) + tile, BF16),
            vmem((2, 2) + tile, BF16),
            vmem((2, 3, 2) + tile, BF16),
            vmem((2, 2) + tile, BF16),
            vmem((2, 3) + tile, BF16),
            vmem((2, 2, 3) + tile, BF16),
            vmem((TAPS * C, BLOCKS * LANES), F32),
            vmem((2, C * ROWS, LANES), F32),
            vmem((2, C, ROWS, LANES), BF16),
            vmem((TAPS * C, LANES), F32),
            vmem((GROUP, TAPS, LANES), F32),
            vmem((GROUP, TAPS, LANES), F32),
            vmem((TAPS, LANES), F32),
            vmem((ZS, TAPS, LANES), F32),
            vmem((TAPS, LANES), F32),
            dma((7,)),
            dma((2, 2, 2)),
            dma((2, 2, 2)),
            dma((3, 3)),
            dma((3, 3)),
            dma((2,)),
            dma((2,)),
            dma((3,)),
            dma((3,)),
            dma((3,)),
        ],
        compiler_params=pltpu.CompilerParams(
            collective_id=0, has_side_effects=True, vmem_limit_bytes=60 * 2**20
        ),
    )(
        snapshot.reshape(C, ROWS, LANES),
        cotangent.reshape(C, ROWS, LANES),
        snap_index.reshape(1, 1),
        snap_means.T,
        snap_scales.T,
        out_bias.reshape(1, C),
        weights.transpose(2, 3, 4, 0, 1).reshape(27, C, C),
    )
    pred, sg, kg, bias = pl.pallas_call(
        deliver,
        out_shape=results,
        in_specs=[anywhere] * 3,
        out_specs=(hbm,) * 4,
        scratch_shapes=[
            vmem((C, ROWS, LANES), BF16),
            vmem((C, ROWS, LANES), BF16),
            vmem((GROUP, TAPS, LANES), F32),
            vmem((27, C, C), F32),
            vmem((1, C), F32),
            dma((3,)),
            dma((4,)),
        ],
        compiler_params=pltpu.CompilerParams(vmem_limit_bytes=60 * 2**20),
    )(*computed)
    return (
        pred.reshape(C, 1, ROWS, LANES),
        sg.reshape(C, 1, ROWS, LANES),
        kg.reshape(3, 3, 3, C, C).transpose(3, 4, 0, 1, 2),
        bias.reshape(C),
    )


def solution(mesh):
    split = P(None, "gx", "gy", "gz")
    in_specs = (split, P(), P(), P(), P(), P(), split)
    out_specs = (split, split, P(), P())
    return jax.shard_map(body, mesh=mesh, in_specs=in_specs, out_specs=out_specs, check_vma=False)
```

```python
import functools
import math

import jax
import jax.numpy as jnp
from jax import lax
from jax.experimental import pallas as pl
from jax.experimental.pallas import tpu as pltpu
from jax.sharding import PartitionSpec as P

F32 = jnp.float32
BF16 = jnp.bfloat16
MESH = pl.DeviceIdType.MESH
C = 32
ROWS = 32
LANES = 128
TAPS = 9
PLANES = 16
ZS = 8
GROUP = 32
BLOCKS = 35
HALF = ROWS // 2
HALO = 34
TOP, BOTTOM = 0, 33
LEFT, RIGHT = 0, 64


def block(b):
    return pl.ds(b * LANES, LANES)


def kernel(
    scale,
    snap, cot, idx_in, means_in, scales_in, bias_in, weights,
    o_pred, o_sg, o_sum,
    raw_own, raw_n, raw_c, w_raw, idx, means, scales, bias, flat, xn, xc, d, wp, ws,
    edge, side, edge_in, side_in, pack, pack_in,
    res, out32, out16, kg_acc, kg_own, rs_in, z_own, z_in, total_own,
    s_load, s_bulk, r_bulk, s_halo, r_halo, s_pack, r_pack, s_sum, r_sum, s_out,
):
    gx, gy, gz = lax.axis_index("gx"), lax.axis_index("gy"), lax.axis_index("gz")
    ring, high = lax.rem(gx, ZS), gx // ZS
    me = high * 16 + gy * 4 + gz

    def member(k):
        return {"gx": (k // 16) * ZS + ring, "gy": lax.rem(k // 4, 4), "gz": lax.rem(k, 4)}

    def along(k):
        return {"gx": high * ZS + k}

    loads = [
        pltpu.make_async_copy(snap, raw_own.at[0], s_load.at[0]),
        pltpu.make_async_copy(cot, raw_own.at[1], s_load.at[1]),
        pltpu.make_async_copy(weights, w_raw, s_load.at[2]),
        pltpu.make_async_copy(idx_in, idx, s_load.at[3]),
        pltpu.make_async_copy(means_in, means, s_load.at[4]),
        pltpu.make_async_copy(scales_in, scales, s_load.at[5]),
        pltpu.make_async_copy(bias_in, bias, s_load.at[6]),
    ]
    loads[0].start()

    next_x = [lax.rem(gx + 1, PLANES), lax.rem(gx + PLANES - 1, PLANES)]
    barrier = pltpu.get_barrier_semaphore()
    for x in next_x:
        pl.semaphore_signal(barrier, inc=1, device_id={"gx": x}, device_id_type=MESH)
    for k in range(1, ZS):
        pl.semaphore_signal(barrier, inc=1, device_id=along(lax.rem(ring + k, ZS)), device_id_type=MESH)
    for k in range(1, GROUP):
        pl.semaphore_signal(barrier, inc=1, device_id=member(lax.rem(me + k, GROUP)), device_id_type=MESH)
    pl.semaphore_wait(barrier, 2 + ZS - 1 + GROUP - 1)

    def bulk(field, source, landing):
        copies = []
        for half in range(2):
            for way in range(2):
                copies.append(
                    pltpu.make_async_remote_copy(
                        source.at[:, pl.ds(half * HALF, HALF)], landing.at[way, half],
                        s_bulk.at[field, way, half], r_bulk.at[field, way, half],
                        device_id={"gx": next_x[way]}, device_id_type=MESH,
                    )
                )
        return copies

    bulk_n = bulk(0, snap, raw_n)
    bulk_c = bulk(1, cot, raw_c)
    for copy in bulk_n:
        copy.start()
    for i in (4, 5, 3, 1, 2, 6):
        loads[i].start()

    for copy in loads[3:]:
        copy.wait()
    chosen = lax.broadcasted_iota(jnp.int32, means.shape, 1) == idx[...]
    centre = jnp.sum(jnp.where(chosen, means[...], 0.0), 1, keepdims=True)
    spread = 1.0 / jnp.sum(jnp.where(chosen, scales[...], 0.0), 1, keepdims=True)
    centre_b = jnp.broadcast_to(centre, (C, LANES))
    spread_b = jnp.broadcast_to(spread, (C, LANES))
    lane = lax.broadcasted_iota(jnp.int32, (C, LANES), 1)

    def relayout(raw, flat, into, row0, start, rows, normalise, edges):
        for c in range(0, C, 8):
            flat[pl.ds(c * rows, 8 * rows), :] = raw[pl.ds(c, 8)].astype(F32).reshape(8 * rows, LANES)
        last = first = jnp.zeros((C, LANES), F32)
        for k in range(rows):
            y = start + k
            v = flat[pl.ds(k, C, stride=rows), :]
            if normalise:
                v = (v - centre_b) * spread_b
            into[pl.ds(row0, C), block(y + 1)] = v.astype(BF16)
            if edges:
                last = jnp.where(lane == LEFT + 1 + y, pltpu.roll(v, y + LEFT + 2, 1), last)
                first = jnp.where(lane == RIGHT + 1 + y, pltpu.roll(v, y + RIGHT + 1, 1), first)
        return last, first

    fields = (xn, xc)
    for f in range(2):
        loads[f].wait()
        last, first = relayout(raw_own.at[f], flat.at[f], fields[f], C, 0, ROWS, f == 0, True)
        side[0, f] = last.astype(BF16)
        side[1, f] = first.astype(BF16)
        edge[0, f] = fields[f][pl.ds(C, C), block(1)]
        edge[1, f] = fields[f][pl.ds(C, C), block(ROWS)]

    halo = []
    for e in range(2):
        y = lax.rem(gy + (3 if e == 0 else 1), 4)
        for k in range(3):
            z = lax.rem(gz + k + 3, 4)
            halo.append(
                pltpu.make_async_remote_copy(
                    edge.at[e], edge_in.at[e, 2 - k], s_halo.at[e, k], r_halo.at[e, 2 - k],
                    device_id={"gy": y, "gz": z}, device_id_type=MESH,
                )
            )
    for k in range(2):
        z = lax.rem(gz + (1 if k == 0 else 3), 4)
        halo.append(
            pltpu.make_async_remote_copy(
                side.at[k], side_in.at[k], s_halo.at[2, k], r_halo.at[2, k],
                device_id={"gz": z}, device_id_type=MESH,
            )
        )
    for copy in halo:
        copy.start()

    loads[2].wait()
    rows_i = lax.broadcasted_iota(jnp.int32, (C, 3 * C), 0)
    cols_i = lax.broadcasted_iota(jnp.int32, (C, 3 * C), 1)
    places = [(cols_i == rows_i + a * C).astype(BF16) for a in range(3)]
    eye = (lax.broadcasted_iota(jnp.int32, (C, C), 0) == lax.broadcasted_iota(jnp.int32, (C, C), 1)).astype(BF16)
    for be in range(TAPS):
        total = jnp.zeros((C, 3 * C), F32)
        for a in range(3):
            total = total + jnp.dot(w_raw[a * TAPS + be], places[a], preferred_element_type=F32)
        wp[pl.ds(be * C, C), :] = total.astype(BF16)
        stack = jnp.concatenate([w_raw[(2 - a) * TAPS + TAPS - 1 - be] for a in range(3)], 0)
        turned = lax.dot_general(eye, stack, (((1,), (1,)), ((), ())), preferred_element_type=F32)
        ws[pl.ds(be * C, C), :] = turned.astype(BF16)
    xn[pl.ds(3 * C, C), :] = jnp.ones((C, BLOCKS * LANES), BF16)

    for copy in halo:
        copy.wait()
    above = (gy > 0).astype(F32)
    below = (gy < 3).astype(F32)
    halo_c = None
    for f in range(2):
        row_top = edge_in[1, 1, f].astype(F32) * above
        row_bottom = edge_in[0, 1, f].astype(F32) * below
        h = side_in[0, f].astype(F32) + side_in[1, f].astype(F32)
        h = jnp.where(lane == LEFT, pltpu.roll(edge_in[1, 0, f].astype(F32) * above, LEFT + 1, 1), h)
        h = jnp.where(lane == LEFT + 33, pltpu.roll(edge_in[0, 0, f].astype(F32) * below, LEFT + 34, 1), h)
        h = jnp.where(lane == RIGHT, pltpu.roll(edge_in[1, 2, f].astype(F32) * above, RIGHT, 1), h)
        h = jnp.where(lane == RIGHT + 33, pltpu.roll(edge_in[0, 2, f].astype(F32) * below, RIGHT + 33, 1), h)
        for i, (b, v) in enumerate(((TOP, row_top), (BOTTOM, row_bottom), (HALO, h))):
            v16 = v.astype(BF16)
            fields[f][pl.ds(C, C), block(b)] = v16
            pack[f, i] = v16
        if f == 1:
            halo_c = h
    packs = []
    for way in range(2):
        packs.append(
            pltpu.make_async_remote_copy(
                pack, pack_in.at[way], s_pack.at[way], r_pack.at[way],
                device_id={"gx": next_x[way]}, device_id_type=MESH,
            )
        )
    for copy in packs:
        copy.start()

    for r in range(ROWS + 2):
        v16 = xc[pl.ds(C, C), block(r)]
        v = v16.astype(F32)
        up = jnp.where(lane == LANES - 1, pltpu.roll(halo_c, LANES - 1 - RIGHT - r, 1), pltpu.roll(v, LANES - 1, 1))
        down = jnp.where(lane == 0, pltpu.roll(halo_c, (LANES - LEFT - r) % LANES, 1), pltpu.roll(v, 1, 1))
        d[pl.ds(0, C), block(r)] = up.astype(BF16)
        d[pl.ds(C, C), block(r)] = v16
        d[pl.ds(2 * C, C), block(r)] = down.astype(BF16)

    span = HALF * LANES
    total = None
    for half in range(2):
        for way in range(2):
            bulk_n[2 * half + way].wait()
        for way in range(2):
            relayout(
                raw_n.at[way, half], flat.at[way, pl.ds(half * C * HALF, C * HALF)],
                xn, way * 2 * C, half * HALF, HALF, True, False,
            )
        start = half * span
        left = jnp.concatenate([d[:, pl.ds(start + (2 - b) * LANES, span)] for b in range(3)], 0)
        right = xn[:, pl.ds(start + LANES, span)]
        part = lax.dot_general(left, right, (((1,), (1,)), ((), ())), preferred_element_type=F32)
        if half == 0:
            kg_acc[...] = part
        else:
            kg_acc[...] += part
    for be in range(TAPS):
        kg_own[:, be, :] = kg_acc[pl.ds(be * C, C), :]

    near = {0: 0, 1: 1, 2: 2, 3: 1}
    steps = [(dy, dc, dx) for dy in range(4) for dc in range(2) for dx in range(4)][1:]
    steps.sort(key=lambda t: -(4 * (near[t[0]] + near[t[2]]) + t[1]))
    y, core = high * 2 + gy // 2, lax.rem(gy, 2)
    group_peers = [
        lax.rem(y + dy, 4) * 8 + lax.rem(core + dc, 2) * 4 + lax.rem(gz + dx, 4) for dy, dc, dx in steps
    ]
    ring_peers = [lax.rem(ring + k, ZS) for k in (4, 3, 5, 2, 6, 1, 7)]

    def spread_out(source, landing, slot, stage, peers, device):
        for peer in peers:
            pltpu.make_async_remote_copy(
                source(peer), landing.at[slot], s_sum.at[stage], r_sum.at[stage],
                device_id=device(peer), device_id_type=MESH,
            ).start()

    def arrived(landing, stage, count):
        all_of = landing.at[pl.ds(0, count - 1)]
        pltpu.make_async_copy(all_of, all_of, r_sum.at[stage]).wait()
        pltpu.make_async_copy(all_of, all_of, s_sum.at[stage]).wait()

    spread_out(lambda p: kg_own.at[p], rs_in, me, 0, group_peers, member)
    for copy in bulk_c[:2]:
        copy.start()
    rs_in[me] = kg_own[me]

    def of(b, e):
        return pl.ds((b * 3 + e) * C, C)

    def multiply(x, filters, first, count):
        at = pl.ds(first * LANES, count * LANES)
        res[:, at] = jnp.dot(filters[...], x[pl.ds(0, 3 * C), at], preferred_element_type=F32)

    def add_up(finish, field, first, last):
        left = res[of(0, 0), block(HALO)]
        right = res[of(0, 2), block(HALO)]
        for b in range(1, 3):
            left = left + pltpu.roll(res[of(b, 0), block(HALO)], LANES - b, 1)
            right = right + pltpu.roll(res[of(b, 2), block(HALO)], LANES - b, 1)
        for y in range(first, last):
            s = [sum(res[of(b, e), block(y + b)] for b in range(3)) for e in range(3)]
            from_left = jnp.where(lane == 0, pltpu.roll(left, (LANES - y) % LANES, 1), pltpu.roll(s[0], 1, 1))
            from_right = jnp.where(
                lane == LANES - 1, pltpu.roll(right, LANES - 1 - RIGHT - y, 1), pltpu.roll(s[2], LANES - 1, 1)
            )
            out32[field, pl.ds(y, C, stride=ROWS), :] = finish(s[1] + from_left + from_right)

    def write(target, field):
        for c in range(0, C, 8):
            out16[field, pl.ds(c, 8)] = out32[field, pl.ds(c * ROWS, 8 * ROWS), :].reshape(8, ROWS, LANES).astype(BF16)
        copy = pltpu.make_async_copy(out16.at[field], target, s_out.at[field])
        copy.start()
        return copy

    arrived(rs_in, 0, GROUP)
    total = rs_in[0]
    for k in range(1, GROUP):
        total = total + rs_in[k]
    z_own[...] = total
    spread_out(lambda p: z_own, z_in, ring, 1, ring_peers, along)
    for copy in bulk_c[2:]:
        copy.start()
    z_in[ring] = total

    arrived(z_in, 1, ZS)
    total = z_in[0]
    for k in range(1, ZS):
        total = total + z_in[k]
    total_own[...] = total * scale
    spread_out(lambda p: total_own, o_sum, me, 2, group_peers, member)
    mine = pltpu.make_async_copy(total_own, o_sum.at[me], s_out.at[2])
    mine.start()
    for copy in packs:
        copy.wait()
    for way in range(2):
        for f in range(2):
            for i, b in enumerate((TOP, BOTTOM, HALO)):
                fields[f][pl.ds(way * 2 * C, C), block(b)] = pack_in[way, f, i]

    eye32 = lax.broadcasted_iota(jnp.int32, (C, C), 0) == lax.broadcasted_iota(jnp.int32, (C, C), 1)
    bias_col = jnp.sum(jnp.where(eye32, jnp.broadcast_to(bias[...], (C, C)), 0.0), 1, keepdims=True)
    bias_b = jnp.broadcast_to(bias_col, (C, LANES))
    multiply(xn, wp, 0, BLOCKS)
    add_up(lambda v: v + bias_b, 0, 0, ROWS)
    written = [write(o_pred, 0)]

    for copy in bulk_c[:2]:
        copy.wait()
    for way in range(2):
        relayout(
            raw_c.at[way, 0], flat.at[way, pl.ds(0, C * HALF)],
            xc, way * 2 * C, 0, HALF, False, False,
        )
    multiply(xc, ws, 0, HALF + 1)
    multiply(xc, ws, HALO, 1)
    add_up(lambda v: v * spread_b, 1, 0, HALF - 1)

    for copy in bulk_c[2:]:
        copy.wait()
    for way in range(2):
        relayout(
            raw_c.at[way, 1], flat.at[way, pl.ds(C * HALF, C * HALF)],
            xc, way * 2 * C, HALF, HALF, False, False,
        )
    multiply(xc, ws, HALF + 1, HALF + 1)
    add_up(lambda v: v * spread_b, 1, HALF - 1, ROWS)
    written.append(write(o_sg, 1))
    arrived(o_sum, 2, GROUP)
    mine.wait()
    for copy in written:
        copy.wait()


def deliver(pred, sg, sums, o_pred, o_sg, o_kg, o_bias, pred_v, sg_v, sums_v, kg_v, bias_v, s_in, s_out):
    arrivals = [
        pltpu.make_async_copy(source, target, s_in.at[i])
        for i, (source, target) in enumerate(((sums, sums_v), (pred, pred_v), (sg, sg_v)))
    ]
    for copy in arrivals:
        copy.start()
    departures = [
        pltpu.make_async_copy(source, target, s_out.at[i])
        for i, (source, target) in enumerate(((kg_v, o_kg), (pred_v, o_pred), (sg_v, o_sg), (bias_v, o_bias)))
    ]
    arrivals[0].wait()
    for be in range(TAPS):
        v = sums_v[:, be, :]
        for a in range(3):
            turned = v if a == 0 else pltpu.roll(v, LANES - a * C, 1)
            kg_v[a * TAPS + be] = turned[:, :C]
        if be == 4:
            column = jnp.broadcast_to(v[:, 3 * C : 3 * C + 1], (C, C))
            diagonal = lax.broadcasted_iota(jnp.int32, (C, C), 0) == lax.broadcasted_iota(jnp.int32, (C, C), 1)
            bias_v[...] = jnp.sum(jnp.where(diagonal, column, 0.0), 0, keepdims=True)
    departures[0].start()
    departures[3].start()
    for i in (1, 2):
        arrivals[i].wait()
        departures[i].start()
    for copy in departures:
        copy.wait()


def body(snapshot, snap_index, snap_means, snap_scales, out_bias, weights, cotangent):
    cells = PLANES * 4 * ROWS * 4 * LANES
    scale = 1.0 / math.sqrt(cells)
    shape = jax.ShapeDtypeStruct
    dma = pltpu.SemaphoreType.DMA
    vmem = pltpu.VMEM
    hbm = pl.BlockSpec(memory_space=pltpu.HBM)
    anywhere = pl.BlockSpec(memory_space=pl.ANY)
    tile = (C, LANES)
    results = (
        shape((C, ROWS, LANES), BF16),
        shape((C, ROWS, LANES), BF16),
        shape((27, C, C), F32),
        shape((1, C), F32),
    )
    computed = pl.pallas_call(
        functools.partial(kernel, scale),
        out_shape=results[:2] + (shape((GROUP, TAPS, LANES), F32),),
        in_specs=[hbm] * 7,
        out_specs=(anywhere,) * 3,
        scratch_shapes=[
            vmem((2, C, ROWS, LANES), BF16),
            vmem((2, 2, C, HALF, LANES), BF16),
            vmem((2, 2, C, HALF, LANES), BF16),
            vmem((27, C, C), BF16),
            vmem((1, 1), jnp.int32),
            vmem((C, 64), F32),
            vmem((C, 64), F32),
            vmem((1, C), F32),
            vmem((2, C * ROWS, LANES), F32),
            vmem((4 * C, BLOCKS * LANES), BF16),
            vmem((3 * C, BLOCKS * LANES), BF16),
            vmem((3 * C, BLOCKS * LANES), BF16),
            vmem((TAPS * C, 3 * C), BF16),
            vmem((TAPS * C, 3 * C), BF16),
            vmem((2, 2) + tile, BF16),
            vmem((2, 2) + tile, BF16),
            vmem((2, 3, 2) + tile, BF16),
            vmem((2, 2) + tile, BF16),
            vmem((2, 3) + tile, BF16),
            vmem((2, 2, 3) + tile, BF16),
            vmem((TAPS * C, BLOCKS * LANES), F32),
            vmem((2, C * ROWS, LANES), F32),
            vmem((2, C, ROWS, LANES), BF16),
            vmem((TAPS * C, LANES), F32),
            vmem((GROUP, TAPS, LANES), F32),
            vmem((GROUP, TAPS, LANES), F32),
            vmem((TAPS, LANES), F32),
            vmem((ZS, TAPS, LANES), F32),
            vmem((TAPS, LANES), F32),
            dma((7,)),
            dma((2, 2, 2)),
            dma((2, 2, 2)),
            dma((3, 3)),
            dma((3, 3)),
            dma((2,)),
            dma((2,)),
            dma((3,)),
            dma((3,)),
            dma((3,)),
        ],
        compiler_params=pltpu.CompilerParams(
            collective_id=0, has_side_effects=True, vmem_limit_bytes=60 * 2**20
        ),
    )(
        snapshot.reshape(C, ROWS, LANES),
        cotangent.reshape(C, ROWS, LANES),
        snap_index.reshape(1, 1),
        snap_means.T,
        snap_scales.T,
        out_bias.reshape(1, C),
        weights.transpose(2, 3, 4, 0, 1).reshape(27, C, C),
    )
    pred, sg, kg, bias = pl.pallas_call(
        deliver,
        out_shape=results,
        in_specs=[anywhere] * 3,
        out_specs=(hbm,) * 4,
        scratch_shapes=[
            vmem((C, ROWS, LANES), BF16),
            vmem((C, ROWS, LANES), BF16),
            vmem((GROUP, TAPS, LANES), F32),
            vmem((27, C, C), F32),
            vmem((1, C), F32),
            dma((3,)),
            dma((4,)),
        ],
        compiler_params=pltpu.CompilerParams(vmem_limit_bytes=60 * 2**20),
    )(*computed)
    return (
        pred.reshape(C, 1, ROWS, LANES),
        sg.reshape(C, 1, ROWS, LANES),
        kg.reshape(3, 3, 3, C, C).transpose(3, 4, 0, 1, 2),
        bias.reshape(C),
    )


def solution(mesh):
    split = P(None, "gx", "gy", "gz")
    in_specs = (split, P(), P(), P(), P(), P(), split)
    out_specs = (split, split, P(), P())
    return jax.shard_map(body, mesh=mesh, in_specs=in_specs, out_specs=out_specs, check_vma=False)
```

```python
import functools
import math

import jax
import jax.numpy as jnp
from jax import lax
from jax.experimental import pallas as pl
from jax.experimental.pallas import tpu as pltpu
from jax.sharding import PartitionSpec as P

F32 = jnp.float32
BF16 = jnp.bfloat16
MESH = pl.DeviceIdType.MESH
C = 32
ROWS = 32
LANES = 128
TAPS = 9
PLANES = 16
ZS = 8
GROUP = 32
BLOCKS = 35
HALF = ROWS // 2
HALO = 34
TOP, BOTTOM = 0, 33
LEFT, RIGHT = 0, 64


def block(b):
    return pl.ds(b * LANES, LANES)


def kernel(
    scale,
    snap, cot, idx_in, means_in, scales_in, bias_in, weights,
    o_pred, o_sg, o_sum,
    raw_own, raw_n, raw_c, w_raw, idx, means, scales, bias, flat, xn, xc, d, wp, ws,
    edge, side, edge_in, side_in, pack, pack_in,
    res, out32, out16, kg_acc, kg_own, rs_in, z_own, z_in, total_own,
    s_load, s_bulk, r_bulk, s_halo, r_halo, s_pack, r_pack, s_sum, r_sum, s_out,
):
    gx, gy, gz = lax.axis_index("gx"), lax.axis_index("gy"), lax.axis_index("gz")
    ring, high = lax.rem(gx, ZS), gx // ZS
    me = high * 16 + gy * 4 + gz

    def member(k):
        return {"gx": (k // 16) * ZS + ring, "gy": lax.rem(k // 4, 4), "gz": lax.rem(k, 4)}

    def along(k):
        return {"gx": high * ZS + k}

    loads = [
        pltpu.make_async_copy(snap, raw_own.at[0], s_load.at[0]),
        pltpu.make_async_copy(cot, raw_own.at[1], s_load.at[1]),
        pltpu.make_async_copy(weights, w_raw, s_load.at[2]),
        pltpu.make_async_copy(idx_in, idx, s_load.at[3]),
        pltpu.make_async_copy(means_in, means, s_load.at[4]),
        pltpu.make_async_copy(scales_in, scales, s_load.at[5]),
        pltpu.make_async_copy(bias_in, bias, s_load.at[6]),
    ]
    loads[0].start()

    next_x = [lax.rem(gx + 1, PLANES), lax.rem(gx + PLANES - 1, PLANES)]
    barrier = pltpu.get_barrier_semaphore()
    for x in next_x:
        pl.semaphore_signal(barrier, inc=1, device_id={"gx": x}, device_id_type=MESH)
    for k in range(1, ZS):
        pl.semaphore_signal(barrier, inc=1, device_id=along(lax.rem(ring + k, ZS)), device_id_type=MESH)
    for k in range(1, GROUP):
        pl.semaphore_signal(barrier, inc=1, device_id=member(lax.rem(me + k, GROUP)), device_id_type=MESH)
    pl.semaphore_wait(barrier, 2 + ZS - 1 + GROUP - 1)

    def bulk(field, source, landing):
        copies = []
        for half in range(2):
            for way in range(2):
                copies.append(
                    pltpu.make_async_remote_copy(
                        source.at[:, pl.ds(half * HALF, HALF)], landing.at[way, half],
                        s_bulk.at[field, way, half], r_bulk.at[field, way, half],
                        device_id={"gx": next_x[way]}, device_id_type=MESH,
                    )
                )
        return copies

    bulk_n = bulk(0, snap, raw_n)
    bulk_c = bulk(1, cot, raw_c)
    for copy in bulk_n:
        copy.start()
    for i in (4, 5, 3, 1, 2, 6):
        loads[i].start()

    for copy in loads[3:]:
        copy.wait()
    chosen = lax.broadcasted_iota(jnp.int32, means.shape, 1) == idx[...]
    centre = jnp.sum(jnp.where(chosen, means[...], 0.0), 1, keepdims=True)
    spread = 1.0 / jnp.sum(jnp.where(chosen, scales[...], 0.0), 1, keepdims=True)
    centre_b = jnp.broadcast_to(centre, (C, LANES))
    spread_b = jnp.broadcast_to(spread, (C, LANES))
    lane = lax.broadcasted_iota(jnp.int32, (C, LANES), 1)

    def relayout(raw, flat, into, row0, start, rows, normalise, edges):
        for c in range(0, C, 8):
            flat[pl.ds(c * rows, 8 * rows), :] = raw[pl.ds(c, 8)].astype(F32).reshape(8 * rows, LANES)
        last = first = jnp.zeros((C, LANES), F32)
        for k in range(rows):
            y = start + k
            v = flat[pl.ds(k, C, stride=rows), :]
            if normalise:
                v = (v - centre_b) * spread_b
            into[pl.ds(row0, C), block(y + 1)] = v.astype(BF16)
            if edges:
                last = jnp.where(lane == LEFT + 1 + y, pltpu.roll(v, y + LEFT + 2, 1), last)
                first = jnp.where(lane == RIGHT + 1 + y, pltpu.roll(v, y + RIGHT + 1, 1), first)
        return last, first

    fields = (xn, xc)
    for f in range(2):
        loads[f].wait()
        last, first = relayout(raw_own.at[f], flat.at[f], fields[f], C, 0, ROWS, f == 0, True)
        side[0, f] = last.astype(BF16)
        side[1, f] = first.astype(BF16)
        edge[0, f] = fields[f][pl.ds(C, C), block(1)]
        edge[1, f] = fields[f][pl.ds(C, C), block(ROWS)]

    halo = []
    for e in range(2):
        y = lax.rem(gy + (3 if e == 0 else 1), 4)
        for k in range(3):
            z = lax.rem(gz + k + 3, 4)
            halo.append(
                pltpu.make_async_remote_copy(
                    edge.at[e], edge_in.at[e, 2 - k], s_halo.at[e, k], r_halo.at[e, 2 - k],
                    device_id={"gy": y, "gz": z}, device_id_type=MESH,
                )
            )
    for k in range(2):
        z = lax.rem(gz + (1 if k == 0 else 3), 4)
        halo.append(
            pltpu.make_async_remote_copy(
                side.at[k], side_in.at[k], s_halo.at[2, k], r_halo.at[2, k],
                device_id={"gz": z}, device_id_type=MESH,
            )
        )
    for copy in halo:
        copy.start()

    loads[2].wait()
    rows_i = lax.broadcasted_iota(jnp.int32, (C, 3 * C), 0)
    cols_i = lax.broadcasted_iota(jnp.int32, (C, 3 * C), 1)
    places = [(cols_i == rows_i + a * C).astype(BF16) for a in range(3)]
    eye = (lax.broadcasted_iota(jnp.int32, (C, C), 0) == lax.broadcasted_iota(jnp.int32, (C, C), 1)).astype(BF16)
    for be in range(TAPS):
        total = jnp.zeros((C, 3 * C), F32)
        for a in range(3):
            total = total + jnp.dot(w_raw[a * TAPS + be], places[a], preferred_element_type=F32)
        wp[pl.ds(be * C, C), :] = total.astype(BF16)
        stack = jnp.concatenate([w_raw[(2 - a) * TAPS + TAPS - 1 - be] for a in range(3)], 0)
        turned = lax.dot_general(eye, stack, (((1,), (1,)), ((), ())), preferred_element_type=F32)
        ws[pl.ds(be * C, C), :] = turned.astype(BF16)
    xn[pl.ds(3 * C, C), :] = jnp.ones((C, BLOCKS * LANES), BF16)

    for copy in halo:
        copy.wait()
    above = (gy > 0).astype(F32)
    below = (gy < 3).astype(F32)
    halo_c = None
    for f in range(2):
        row_top = edge_in[1, 1, f].astype(F32) * above
        row_bottom = edge_in[0, 1, f].astype(F32) * below
        h = side_in[0, f].astype(F32) + side_in[1, f].astype(F32)
        h = jnp.where(lane == LEFT, pltpu.roll(edge_in[1, 0, f].astype(F32) * above, LEFT + 1, 1), h)
        h = jnp.where(lane == LEFT + 33, pltpu.roll(edge_in[0, 0, f].astype(F32) * below, LEFT + 34, 1), h)
        h = jnp.where(lane == RIGHT, pltpu.roll(edge_in[1, 2, f].astype(F32) * above, RIGHT, 1), h)
        h = jnp.where(lane == RIGHT + 33, pltpu.roll(edge_in[0, 2, f].astype(F32) * below, RIGHT + 33, 1), h)
        for i, (b, v) in enumerate(((TOP, row_top), (BOTTOM, row_bottom), (HALO, h))):
            v16 = v.astype(BF16)
            fields[f][pl.ds(C, C), block(b)] = v16
            pack[f, i] = v16
        if f == 1:
            halo_c = h
    packs = []
    for way in range(2):
        packs.append(
            pltpu.make_async_remote_copy(
                pack, pack_in.at[way], s_pack.at[way], r_pack.at[way],
                device_id={"gx": next_x[way]}, device_id_type=MESH,
            )
        )
    for copy in packs:
        copy.start()

    for r in range(ROWS + 2):
        v16 = xc[pl.ds(C, C), block(r)]
        v = v16.astype(F32)
        up = jnp.where(lane == LANES - 1, pltpu.roll(halo_c, LANES - 1 - RIGHT - r, 1), pltpu.roll(v, LANES - 1, 1))
        down = jnp.where(lane == 0, pltpu.roll(halo_c, (LANES - LEFT - r) % LANES, 1), pltpu.roll(v, 1, 1))
        d[pl.ds(0, C), block(r)] = up.astype(BF16)
        d[pl.ds(C, C), block(r)] = v16
        d[pl.ds(2 * C, C), block(r)] = down.astype(BF16)

    span = HALF * LANES
    total = None
    for half in range(2):
        for way in range(2):
            bulk_n[2 * half + way].wait_recv()
        for way in range(2):
            relayout(
                raw_n.at[way, half], flat.at[way, pl.ds(half * C * HALF, C * HALF)],
                xn, way * 2 * C, half * HALF, HALF, True, False,
            )
        start = half * span
        left = jnp.concatenate([d[:, pl.ds(start + (2 - b) * LANES, span)] for b in range(3)], 0)
        right = xn[:, pl.ds(start + LANES, span)]
        part = lax.dot_general(left, right, (((1,), (1,)), ((), ())), preferred_element_type=F32)
        if half == 0:
            kg_acc[...] = part
    for be in range(TAPS):
        kg_own[:, be, :] = kg_acc[pl.ds(be * C, C), :] + part[be * C : (be + 1) * C]

    near = {0: 0, 1: 1, 2: 2, 3: 1}
    steps = [(dy, dc, dx) for dy in range(4) for dc in range(2) for dx in range(4)][1:]
    steps.sort(key=lambda t: -(4 * (near[t[0]] + near[t[2]]) + t[1]))
    y, core = high * 2 + gy // 2, lax.rem(gy, 2)
    group_peers = [
        lax.rem(y + dy, 4) * 8 + lax.rem(core + dc, 2) * 4 + lax.rem(gz + dx, 4) for dy, dc, dx in steps
    ]
    ring_peers = [lax.rem(ring + k, ZS) for k in (4, 3, 5, 2, 6, 1, 7)]

    def spread_out(source, landing, slot, stage, peers, device):
        for peer in peers:
            pltpu.make_async_remote_copy(
                source(peer), landing.at[slot], s_sum.at[stage], r_sum.at[stage],
                device_id=device(peer), device_id_type=MESH,
            ).start()

    def arrived(landing, stage, count):
        all_of = landing.at[pl.ds(0, count - 1)]
        pltpu.make_async_copy(all_of, all_of, r_sum.at[stage]).wait()

    def sent(landing, stage, count):
        all_of = landing.at[pl.ds(0, count - 1)]
        pltpu.make_async_copy(all_of, all_of, s_sum.at[stage]).wait()

    spread_out(lambda p: kg_own.at[p], rs_in, me, 0, group_peers, member)
    for copy in bulk_c[:2]:
        copy.start()
    rs_in[me] = kg_own[me]

    def of(b, e):
        return pl.ds((b * 3 + e) * C, C)

    def multiply(x, filters, first, count):
        at = pl.ds(first * LANES, count * LANES)
        res[:, at] = jnp.dot(filters[...], x[pl.ds(0, 3 * C), at], preferred_element_type=F32)

    def add_up(finish, field, first, last):
        left = res[of(0, 0), block(HALO)]
        right = res[of(0, 2), block(HALO)]
        for b in range(1, 3):
            left = left + pltpu.roll(res[of(b, 0), block(HALO)], LANES - b, 1)
            right = right + pltpu.roll(res[of(b, 2), block(HALO)], LANES - b, 1)
        for y in range(first, last):
            s = [sum(res[of(b, e), block(y + b)] for b in range(3)) for e in range(3)]
            from_left = jnp.where(lane == 0, pltpu.roll(left, (LANES - y) % LANES, 1), pltpu.roll(s[0], 1, 1))
            from_right = jnp.where(
                lane == LANES - 1, pltpu.roll(right, LANES - 1 - RIGHT - y, 1), pltpu.roll(s[2], LANES - 1, 1)
            )
            out32[field, pl.ds(y, C, stride=ROWS), :] = finish(s[1] + from_left + from_right)

    def write(target, field):
        for c in range(0, C, 8):
            out16[field, pl.ds(c, 8)] = out32[field, pl.ds(c * ROWS, 8 * ROWS), :].reshape(8, ROWS, LANES).astype(BF16)
        copy = pltpu.make_async_copy(out16.at[field], target, s_out.at[field])
        copy.start()
        return copy

    arrived(rs_in, 0, GROUP)
    total = rs_in[0]
    for k in range(1, GROUP):
        total = total + rs_in[k]
    z_own[...] = total
    spread_out(lambda p: z_own, z_in, ring, 1, ring_peers, along)
    for copy in bulk_c[2:]:
        copy.start()
    z_in[ring] = total

    arrived(z_in, 1, ZS)
    total = z_in[0]
    for k in range(1, ZS):
        total = total + z_in[k]
    total_own[...] = total * scale
    spread_out(lambda p: total_own, o_sum, me, 2, group_peers, member)
    mine = pltpu.make_async_copy(total_own, o_sum.at[me], s_out.at[2])
    mine.start()
    for copy in packs:
        copy.wait()
    for way in range(2):
        for f in range(2):
            for i, b in enumerate((TOP, BOTTOM, HALO)):
                fields[f][pl.ds(way * 2 * C, C), block(b)] = pack_in[way, f, i]

    eye32 = lax.broadcasted_iota(jnp.int32, (C, C), 0) == lax.broadcasted_iota(jnp.int32, (C, C), 1)
    bias_col = jnp.sum(jnp.where(eye32, jnp.broadcast_to(bias[...], (C, C)), 0.0), 1, keepdims=True)
    bias_b = jnp.broadcast_to(bias_col, (C, LANES))
    multiply(xn, wp, 0, BLOCKS)
    add_up(lambda v: v + bias_b, 0, 0, ROWS)
    written = [write(o_pred, 0)]

    for copy in bulk_c[:2]:
        copy.wait()
    for way in range(2):
        relayout(
            raw_c.at[way, 0], flat.at[way, pl.ds(0, C * HALF)],
            xc, way * 2 * C, 0, HALF, False, False,
        )
    multiply(xc, ws, 0, HALF + 1)
    multiply(xc, ws, HALO, 1)
    add_up(lambda v: v * spread_b, 1, 0, HALF - 1)

    for copy in bulk_c[2:]:
        copy.wait()
    for way in range(2):
        relayout(
            raw_c.at[way, 1], flat.at[way, pl.ds(C * HALF, C * HALF)],
            xc, way * 2 * C, HALF, HALF, False, False,
        )
    multiply(xc, ws, HALF + 1, HALF + 1)
    add_up(lambda v: v * spread_b, 1, HALF - 1, ROWS)
    written.append(write(o_sg, 1))
    for copy in bulk_n:
        copy.wait_send()
    stages = ((rs_in, 0, GROUP), (z_in, 1, ZS), (o_sum, 2, GROUP))
    for landing, stage, count in stages:
        sent(landing, stage, count)
    arrived(o_sum, 2, GROUP)
    mine.wait()
    for copy in written:
        copy.wait()


def deliver(pred, sg, sums, o_pred, o_sg, o_kg, o_bias, pred_v, sg_v, sums_v, kg_v, bias_v, s_in, s_out):
    arrivals = [
        pltpu.make_async_copy(source, target, s_in.at[i])
        for i, (source, target) in enumerate(((sums, sums_v), (pred, pred_v), (sg, sg_v)))
    ]
    for copy in arrivals:
        copy.start()
    departures = [
        pltpu.make_async_copy(source, target, s_out.at[i])
        for i, (source, target) in enumerate(((kg_v, o_kg), (pred_v, o_pred), (sg_v, o_sg), (bias_v, o_bias)))
    ]
    arrivals[0].wait()
    for be in range(TAPS):
        v = sums_v[:, be, :]
        for a in range(3):
            turned = v if a == 0 else pltpu.roll(v, LANES - a * C, 1)
            kg_v[a * TAPS + be] = turned[:, :C]
        if be == 4:
            column = jnp.broadcast_to(v[:, 3 * C : 3 * C + 1], (C, C))
            diagonal = lax.broadcasted_iota(jnp.int32, (C, C), 0) == lax.broadcasted_iota(jnp.int32, (C, C), 1)
            bias_v[...] = jnp.sum(jnp.where(diagonal, column, 0.0), 0, keepdims=True)
    departures[0].start()
    departures[3].start()
    for i in (1, 2):
        arrivals[i].wait()
        departures[i].start()
    for copy in departures:
        copy.wait()


def body(snapshot, snap_index, snap_means, snap_scales, out_bias, weights, cotangent):
    cells = PLANES * 4 * ROWS * 4 * LANES
    scale = 1.0 / math.sqrt(cells)
    shape = jax.ShapeDtypeStruct
    dma = pltpu.SemaphoreType.DMA
    vmem = pltpu.VMEM
    hbm = pl.BlockSpec(memory_space=pltpu.HBM)
    anywhere = pl.BlockSpec(memory_space=pl.ANY)
    tile = (C, LANES)
    results = (
        shape((C, ROWS, LANES), BF16),
        shape((C, ROWS, LANES), BF16),
        shape((27, C, C), F32),
        shape((1, C), F32),
    )
    computed = pl.pallas_call(
        functools.partial(kernel, scale),
        out_shape=results[:2] + (shape((GROUP, TAPS, LANES), F32),),
        in_specs=[hbm] * 7,
        out_specs=(anywhere,) * 3,
        scratch_shapes=[
            vmem((2, C, ROWS, LANES), BF16),
            vmem((2, 2, C, HALF, LANES), BF16),
            vmem((2, 2, C, HALF, LANES), BF16),
            vmem((27, C, C), BF16),
            vmem((1, 1), jnp.int32),
            vmem((C, 64), F32),
            vmem((C, 64), F32),
            vmem((1, C), F32),
            vmem((2, C * ROWS, LANES), F32),
            vmem((4 * C, BLOCKS * LANES), BF16),
            vmem((3 * C, BLOCKS * LANES), BF16),
            vmem((3 * C, BLOCKS * LANES), BF16),
            vmem((TAPS * C, 3 * C), BF16),
            vmem((TAPS * C, 3 * C), BF16),
            vmem((2, 2) + tile, BF16),
            vmem((2, 2) + tile, BF16),
            vmem((2, 3, 2) + tile, BF16),
            vmem((2, 2) + tile, BF16),
            vmem((2, 3) + tile, BF16),
            vmem((2, 2, 3) + tile, BF16),
            vmem((TAPS * C, BLOCKS * LANES), F32),
            vmem((2, C * ROWS, LANES), F32),
            vmem((2, C, ROWS, LANES), BF16),
            vmem((TAPS * C, LANES), F32),
            vmem((GROUP, TAPS, LANES), F32),
            vmem((GROUP, TAPS, LANES), F32),
            vmem((TAPS, LANES), F32),
            vmem((ZS, TAPS, LANES), F32),
            vmem((TAPS, LANES), F32),
            dma((7,)),
            dma((2, 2, 2)),
            dma((2, 2, 2)),
            dma((3, 3)),
            dma((3, 3)),
            dma((2,)),
            dma((2,)),
            dma((3,)),
            dma((3,)),
            dma((3,)),
        ],
        compiler_params=pltpu.CompilerParams(
            collective_id=0, has_side_effects=True, vmem_limit_bytes=60 * 2**20
        ),
    )(
        snapshot.reshape(C, ROWS, LANES),
        cotangent.reshape(C, ROWS, LANES),
        snap_index.reshape(1, 1),
        snap_means.T,
        snap_scales.T,
        out_bias.reshape(1, C),
        weights.transpose(2, 3, 4, 0, 1).reshape(27, C, C),
    )
    pred, sg, kg, bias = pl.pallas_call(
        deliver,
        out_shape=results,
        in_specs=[anywhere] * 3,
        out_specs=(hbm,) * 4,
        scratch_shapes=[
            vmem((C, ROWS, LANES), BF16),
            vmem((C, ROWS, LANES), BF16),
            vmem((GROUP, TAPS, LANES), F32),
            vmem((27, C, C), F32),
            vmem((1, C), F32),
            dma((3,)),
            dma((4,)),
        ],
        compiler_params=pltpu.CompilerParams(vmem_limit_bytes=60 * 2**20),
    )(*computed)
    return (
        pred.reshape(C, 1, ROWS, LANES),
        sg.reshape(C, 1, ROWS, LANES),
        kg.reshape(3, 3, 3, C, C).transpose(3, 4, 0, 1, 2),
        bias.reshape(C),
    )


def solution(mesh):
    split = P(None, "gx", "gy", "gz")
    in_specs = (split, P(), P(), P(), P(), P(), split)
    out_specs = (split, split, P(), P())
    return jax.shard_map(body, mesh=mesh, in_specs=in_specs, out_specs=out_specs, check_vma=False)
```
